128 devices in a mesh: seq: 8 (over x_lo, z), col: 16 (over y, x_hi, core).
Axes of the slice: x: 4 (x_hi: 2, x_lo: 2; x = x_hi * 2 + x_lo), y: 4, z: 4, core: 2. Of those that a mesh axis runs over, the one named last changes fastest.
Arguments:
- stream: bfloat16 [64, 1024, 768], P('seq', 'col'), may hold values from -40 to 40
- row_mask: int32 [64], replicated, may hold values from 0 to 1, as said below
- gain_row: bfloat16 [768], replicated, may hold values from 0.5 to 1.5
- row_query: bfloat16 [768, 768], replicated, may hold values from -13 to 13
- row_key: bfloat16 [768, 768], replicated, may hold values from -1 to 1
- row_value: bfloat16 [768, 768], replicated, may hold values from -0.875 to 0.875
- row_output: bfloat16 [768, 768], replicated, may hold values from -0.875 to 0.875
- gain_column: bfloat16 [768], replicated, may hold values from 0.5 to 1.5
- column_query: bfloat16 [768, 768], replicated, may hold values from -13 to 13
- column_key: bfloat16 [768, 768], replicated, may hold values from -1 to 1
- column_value: bfloat16 [768, 768], replicated, may hold values from -0.4375 to 0.4375
- column_output: bfloat16 [768, 768], replicated, may hold values from -0.4375 to 0.4375
- gain_feed: bfloat16 [768], replicated, may hold values from 0.5 to 1.5
- up_weight: bfloat16 [768, 3072], replicated, may hold values from -0.21875 to 0.21875
- down_weight: bfloat16 [3072, 768], replicated, may hold values from -0.109375 to 0.109375
Outputs:
- layer_out: bfloat16 [64, 1024, 768], P('seq', 'col')
The draws below stay inside these ranges and needn't reach their ends.
Inputs may be any that keep to these rules, and one draw needn't show every extreme that they name: `row_mask`: sequence 0, the query sequence, is never padded.
All inputs are finite; a program needn't handle non-finite values.
Results may differ from the reference program's by a relative error of at most 0.015.
Values may be sent and summed in bfloat16 or wider, within the bound.
A program may use at most 128 MiB of HBM per device.

```python
import math
import jax
import jax.numpy as jnp
from jax import lax

D = 768
H = 12
FF = 3072
DH = 64
C_DEV = 64
R = 64
C = 1024


def paired_base(key, salt):
    raw = jax.random.normal(jax.random.fold_in(key, salt), (D, D), jnp.float32)
    return jnp.clip(raw, -6.0, 6.0) * D ** (-0.5)


def fresh_weight(key):
    raw = jax.random.normal(key, (D, D), jnp.float32)
    return jnp.clip(raw, -6.0, 6.0) * D ** (-0.5)


def draw_row_key(key, part):
    base = paired_base(key, 101)
    return base.astype(jnp.bfloat16)


def draw_row_query(key, part):
    key = jax.random.fold_in(key, 2)
    noise = fresh_weight(key)
    return noise.astype(jnp.bfloat16)


def draw_column_key(key, part):
    base = paired_base(key, 202)
    return base.astype(jnp.bfloat16)


def draw_column_query(key, part):
    key = jax.random.fold_in(key, 4)
    noise = fresh_weight(key)
    return noise.astype(jnp.bfloat16)


def draw_stream(key, part):
    key = jax.random.fold_in(key, 5)
    token_scale = jnp.exp(jax.random.uniform(jax.random.fold_in(key, 1), (R, C, 1), jnp.float32, -1.2, 1.1))
    feature_scale = jnp.exp(jax.random.uniform(jax.random.fold_in(key, 2), (D,), jnp.float32, -1.2, 1.1))
    core = jnp.clip(jax.random.normal(jax.random.fold_in(key, 3), (R, C, D), jnp.float32), -4.0, 4.0)
    return (core * token_scale * feature_scale).astype(jnp.bfloat16)


def draw_row_mask(key, part):
    key = jax.random.fold_in(key, 6)
    levels = jax.random.randint(key, (R,), 0, 5)
    position = jnp.arange(R, dtype=jnp.int32)
    return jnp.where((levels > 0) | (position == 0), 1, 0).astype(jnp.int32)


def centred(rng, shape, scale, most, kind=jnp.bfloat16):
    return jnp.clip(scale * jax.random.normal(rng, shape, jnp.float32), -most, most).astype(kind)


def setup_inputs(seed: int = 0) -> dict:
    key_list = jax.random.split(jax.random.key(seed), 16)
    return {
        "stream": draw_stream(jax.random.fold_in(key_list[15], 71), 0),
        "row_mask": draw_row_mask(jax.random.fold_in(key_list[15], 71), 0),
        "gain_row": jnp.clip(1.0 + 0.1 * jax.random.normal(key_list[2], (D,), jnp.float32), 0.5, 1.5).astype(jnp.bfloat16),
        "row_query": draw_row_query(jax.random.fold_in(key_list[15], 71), 0),
        "row_key": draw_row_key(jax.random.fold_in(key_list[15], 71), 0),
        "row_value": centred(key_list[5], (D, D), (D // 16) ** -0.5, 0.875),
        "row_output": centred(key_list[6], (D, D), (D // 16) ** -0.5, 0.875),
        "gain_column": jnp.clip(1.0 + 0.1 * jax.random.normal(key_list[7], (D,), jnp.float32), 0.5, 1.5).astype(jnp.bfloat16),
        "column_query": draw_column_query(jax.random.fold_in(key_list[15], 71), 0),
        "column_key": draw_column_key(jax.random.fold_in(key_list[15], 71), 0),
        "column_value": centred(key_list[10], (D, D), (D // 4) ** -0.5, 0.4375),
        "column_output": centred(key_list[11], (D, D), (D // 4) ** -0.5, 0.4375),
        "gain_feed": jnp.clip(1.0 + 0.1 * jax.random.normal(key_list[12], (D,), jnp.float32), 0.5, 1.5).astype(jnp.bfloat16),
        "up_weight": centred(key_list[13], (D, FF), D ** -0.5, 0.21875),
        "down_weight": centred(key_list[14], (FF, D), FF ** -0.5, 0.109375),
    }


def layer_norm(values, gain):
    wide = values.astype(jnp.float32)
    center = wide - lax.optimization_barrier(jnp.mean(wide, axis=-1, keepdims=True))
    spread = lax.optimization_barrier(jnp.mean(center * center, axis=-1, keepdims=True))
    return center * lax.rsqrt(spread + 1e-05) * gain.astype(jnp.float32)

def column_attend(queries, key_rows, value_rows, row_mask):
    query_heads = queries.reshape(queries.shape[0], queries.shape[1], H, DH).astype(jnp.float32)
    key_heads = key_rows.reshape(key_rows.shape[0], key_rows.shape[1], H, DH).astype(jnp.float32)
    value_heads = value_rows.reshape(value_rows.shape[0], value_rows.shape[1], H, DH).astype(jnp.float32)
    scores = jnp.einsum('rchd,schd->chrs', query_heads, key_heads) * (1.0 / math.sqrt(DH))
    live_keys = row_mask[None, None, None, :] > 0
    row_max = lax.optimization_barrier(jnp.max(jnp.where(live_keys, scores, -1e+30), axis=-1, keepdims=True))
    exponent = jnp.where(live_keys, jnp.exp(scores - row_max), 0.0)
    softmax_weights = (exponent / lax.optimization_barrier(jnp.sum(exponent, axis=-1, keepdims=True))).astype(jnp.bfloat16)
    result = jnp.einsum('chrs,schd->rchd', softmax_weights.astype(jnp.float32), value_heads)
    return result.astype(jnp.bfloat16).reshape(queries.shape)

def reference(stream, row_mask, gain_row, row_query, row_key, row_value, row_output, gain_column, column_query, column_key, column_value, column_output, gain_feed, up_weight, down_weight):
    flat_rows = stream.reshape(R * C, D)
    normed = layer_norm(flat_rows, gain_row).astype(jnp.bfloat16)

    def project(inputs, weight):
        return jnp.dot(inputs, weight, preferred_element_type=jnp.float32).astype(jnp.bfloat16)
    keep_rows = jnp.repeat(row_mask, C).astype(jnp.bfloat16)[:, None]
    queries = (project(normed, row_query) * keep_rows).reshape(R, C, H, DH)
    key_rows = project(normed, row_key).reshape(R, C, H, DH)
    value_rows = project(normed, row_value).reshape(R, C, H, DH)
    tied = jnp.einsum('rihd,rjhd->hij', queries.astype(jnp.float32), key_rows.astype(jnp.float32))
    tied = tied * (1.0 / math.sqrt(DH * R))
    weights = jax.nn.softmax(tied, axis=-1).astype(jnp.bfloat16)
    row_mixed = jnp.einsum('hij,rjhd->rihd', weights.astype(jnp.float32), value_rows.astype(jnp.float32))
    row_mixed = row_mixed.astype(jnp.bfloat16).reshape(R * C, D)
    after_row = (flat_rows.astype(jnp.float32) + jnp.dot(row_mixed, row_output, preferred_element_type=jnp.float32)).astype(jnp.bfloat16)
    column_in = layer_norm(after_row, gain_column).astype(jnp.bfloat16)
    blocks = C // C_DEV

    def to_blocks(values):
        return jnp.transpose(values.reshape(R, blocks, C_DEV, D), (1, 0, 2, 3))
    column_queries = to_blocks(project(column_in, column_query))
    column_keys = to_blocks(project(column_in, column_key))
    column_values = to_blocks(project(column_in, column_value))

    def one_block(triple):
        return column_attend(triple[0], triple[1], triple[2], row_mask)
    column_mixed = lax.map(one_block, (column_queries, column_keys, column_values))
    column_mixed = jnp.transpose(column_mixed, (1, 0, 2, 3)).reshape(R * C, D)
    after_column = (after_row.astype(jnp.float32) + jnp.dot(column_mixed, column_output, preferred_element_type=jnp.float32)).astype(jnp.bfloat16)
    feed_in = layer_norm(after_column, gain_feed).astype(jnp.bfloat16)
    hidden = jax.nn.gelu(jnp.dot(feed_in, up_weight, preferred_element_type=jnp.float32), approximate=False).astype(jnp.bfloat16)
    layer_out = after_column.astype(jnp.float32) + jnp.dot(hidden, down_weight, preferred_element_type=jnp.float32)
    return layer_out.astype(jnp.bfloat16).reshape(R, C, D)
```

```python
import math

import jax
import jax.numpy as jnp
from jax import lax
from jax.sharding import PartitionSpec as P

H = 12
DH = 64
Y_GROUPS = [[y * 4 + w for y in range(4)] for w in range(4)]
W_GROUPS = [[y * 4 + w for w in range(4)] for y in range(4)]


def layer_norm(values, gain):
    wide = values.astype(jnp.float32)
    center = wide - jnp.mean(wide, axis=-1, keepdims=True)
    spread = jnp.mean(center * center, axis=-1, keepdims=True)
    return center * lax.rsqrt(spread + 1e-05) * gain.astype(jnp.float32)


def dot(a, b):
    return jnp.dot(a, b, preferred_element_type=jnp.float32)


def local(
    stream,
    row_mask,
    gain_row,
    row_query,
    row_key,
    row_value,
    row_output,
    gain_column,
    column_query,
    column_key,
    column_value,
    column_output,
    gain_feed,
    up_weight,
    down_weight,
):
    rows, cols, width = stream.shape
    total = row_mask.shape[0]
    tokens = rows * cols
    hg = H // 4
    gw = hg * DH
    mask_here = lax.dynamic_slice_in_dim(row_mask, lax.axis_index("seq") * rows, rows, 0)
    flat = stream.reshape(tokens, width)
    normed = layer_norm(flat, gain_row).astype(jnp.bfloat16)

    def to_heads(weight, mask=None):
        out = dot(normed, weight).astype(jnp.bfloat16)
        if mask is not None:
            out = (out.reshape(rows, cols, width) * mask[:, None, None]).reshape(tokens, width)
        out = out.reshape(rows, cols, 4, gw).transpose(2, 0, 1, 3)
        return lax.all_to_all(out, "col", 0, 0, axis_index_groups=Y_GROUPS, tiled=True)

    q = to_heads(row_query, mask_here.astype(jnp.bfloat16))
    k = to_heads(row_key)
    v = to_heads(row_value)
    kk = lax.all_gather(k, "col", axis=0, axis_index_groups=W_GROUPS)
    vv = lax.all_gather(v, "col", axis=0, axis_index_groups=W_GROUPS)
    q5 = q.reshape(4, rows, cols, hg, DH)
    k5 = kk.reshape(4, 4, rows, cols, hg, DH)
    v5 = vv.reshape(4, 4, rows, cols, hg, DH)
    part = jnp.einsum("yrihd,wxrjhd->hyiwxj", q5, k5, preferred_element_type=jnp.float32)
    part = part.reshape(hg, 4 * cols, 16 * cols)
    tied = lax.psum_scatter(part, "seq", scatter_dimension=1, tiled=True)
    tied = tied * (1.0 / math.sqrt(DH * total))
    weights = jax.nn.softmax(tied, axis=-1).astype(jnp.bfloat16)
    weights = lax.all_gather(weights, "seq", axis=1, tiled=True)
    weights = weights.reshape(hg, 4, cols, 4, 4, cols)
    mixed = jnp.einsum("hyiwxj,wxrjhd->yrihd", weights, v5, preferred_element_type=jnp.float32)
    mixed = mixed.astype(jnp.bfloat16).reshape(4, rows, cols, gw)
    mixed = lax.all_to_all(mixed, "col", 0, 0, axis_index_groups=Y_GROUPS, tiled=True)
    mixed = mixed.transpose(1, 2, 0, 3).reshape(tokens, width)
    after_row = (flat.astype(jnp.float32) + dot(mixed, row_output)).astype(jnp.bfloat16)

    ns = total // rows
    cl = cols // ns
    moved = after_row.reshape(rows, ns, cl, width).transpose(1, 2, 0, 3)
    moved = lax.all_to_all(moved, "seq", 0, 0, tiled=True)
    x = moved.transpose(1, 0, 2, 3).reshape(tokens, width)
    column_in = layer_norm(x, gain_column).astype(jnp.bfloat16)
    cq = dot(column_in, column_query).astype(jnp.bfloat16).reshape(cl, total, H, DH)
    ck = dot(column_in, column_key).astype(jnp.bfloat16).reshape(cl, total, H, DH)
    cv = dot(column_in, column_value).astype(jnp.bfloat16).reshape(cl, total, H, DH)
    scores = jnp.einsum("crhd,cshd->chrs", cq, ck, preferred_element_type=jnp.float32) * (
        1.0 / math.sqrt(DH)
    )
    live = row_mask[None, None, None, :] > 0
    top = jnp.max(jnp.where(live, scores, -1e30), axis=-1, keepdims=True)
    ex = jnp.where(live, jnp.exp(scores - top), 0.0)
    cw = (ex / jnp.sum(ex, axis=-1, keepdims=True)).astype(jnp.bfloat16)
    cm = jnp.einsum("chrs,cshd->crhd", cw, cv, preferred_element_type=jnp.float32)
    cm = cm.astype(jnp.bfloat16).reshape(tokens, width)
    after_column = (x.astype(jnp.float32) + dot(cm, column_output)).astype(jnp.bfloat16)
    feed_in = layer_norm(after_column, gain_feed).astype(jnp.bfloat16)
    hidden = jax.nn.gelu(dot(feed_in, up_weight), approximate=False).astype(jnp.bfloat16)
    out = (after_column.astype(jnp.float32) + dot(hidden, down_weight)).astype(jnp.bfloat16)
    out = out.reshape(cl, ns, rows, width).transpose(1, 0, 2, 3)
    out = lax.all_to_all(out, "seq", 0, 0, tiled=True)
    return out.transpose(2, 0, 1, 3).reshape(rows, cols, width)


def solution(mesh):
    return jax.shard_map(
        local,
        mesh=mesh,
        in_specs=(P("seq", "col", None),) + (P(),) * 14,
        out_specs=P("seq", "col", None),
        check_vma=False,
    )
```

```python
import functools

import jax
import jax.numpy as jnp
from jax import lax
from jax.experimental import pallas as pl
from jax.experimental.pallas import tpu as pltpu
from jax.sharding import PartitionSpec as P

D = 768
H = 12
DH = 64
FF = 3072
RL = 8
CL = 64
T = RL * CL
NS = 8
NY = 4
NW = 4
HG = H // NY
BF = jnp.bfloat16
F32 = jnp.float32
MESH = pl.DeviceIdType.MESH
VMEM_LIMIT = 56 * 1024 * 1024


def norm(wide, gain):
    center = wide - jnp.mean(wide, axis=-1, keepdims=True)
    spread = jnp.mean(center * center, axis=-1, keepdims=True)
    return center * lax.rsqrt(spread + 1e-05) * gain


def dot(a, b, dims=((1,), (0,))):
    return lax.dot_general(a, b, (dims, ((), ())), preferred_element_type=F32)


def place():
    s = lax.axis_index("seq")
    col = lax.axis_index("col")
    return s, lax.div(col, NW), lax.rem(col, NW)


def remote(src, dst, send, recv, s, col):
    return pltpu.make_async_remote_copy(
        src_ref=src, dst_ref=dst, send_sem=send, recv_sem=recv, device_id=(s, col), device_id_type=MESH
    )


def greet(peers):
    barrier = pltpu.get_barrier_semaphore()
    for s, col in peers:
        pl.semaphore_signal(barrier, inc=1, device_id=(s, col), device_id_type=MESH)
    pl.semaphore_wait(barrier, len(peers))


def pair_lanes(a, b):
    low = lax.broadcasted_iota(jnp.int32, a.shape, 1) < DH
    return jnp.where(low, a, pltpu.roll(b, DH, 1)), jnp.where(low, pltpu.roll(a, DH, 1), b)


def row_kernel(
    mask, x, gain, wq_h, wk_h, wv_h, wo_h, out,
    wk, wq, wv, wo, xn, acc, pk, qb, kb, vb, part, rs, pw, mxs, mxr, cs,
    wsem, ysend, yrecv, wsend, wrecv, rsend, rrecv, psend, precv, msend, mrecv, csend, crecv,
):
    s, y, w = place()
    col = y * NW + w
    ycol = [None] + [lax.rem(y + d, NY) * NW + w for d in range(1, NY)]
    yidx = [None] + [lax.rem(y + d, NY) for d in range(1, NY)]
    sidx = [None] + [lax.rem(s + d, NS) for d in range(1, NS)]
    w_far = lax.rem(w + 2, NW)
    w_core = w + 1 - 2 * lax.rem(w, 2)
    w_diag = lax.rem(w_core + 2, NW)
    far, core = y * NW + w_far, y * NW + w_core

    loads = []
    for i, (h, v) in enumerate(((wk_h, wk), (wq_h, wq), (wv_h, wv), (wo_h, wo))):
        loads.append(pltpu.make_async_copy(h, v, wsem.at[i]))
        loads[-1].start()
    greet([(s, c) for c in ycol[1:]] + [(s, far), (s, core)] + [(d, col) for d in sidx[1:]])

    xn[...] = norm(x[...].astype(F32), gain[...].astype(F32)).astype(BF)
    sends = []

    def project(kind, weight, load, into, base, masked=False):
        load.wait()
        acc[...] = dot(xn[...], weight[...])
        for p in range(RL // 2):
            for hp in range(H // 2):
                a = acc[2 * p * CL:(2 * p + 1) * CL, hp * 128:(hp + 1) * 128]
                b = acc[(2 * p + 1) * CL:(2 * p + 2) * CL, hp * 128:(hp + 1) * 128]
                if masked:
                    a = a * mask[s * RL + 2 * p].astype(F32)
                    b = b * mask[s * RL + 2 * p + 1].astype(F32)
                first, second = pair_lanes(a, b)
                pk[kind, 2 * hp, :, p * 128:(p + 1) * 128] = first.astype(BF)
                pk[kind, 2 * hp + 1, :, p * 128:(p + 1) * 128] = second.astype(BF)
        rows = pl.ds(pl.multiple_of(base, CL), CL)
        copies = []
        for g in range(HG):
            group = []
            for d in range(1, NY):
                c = remote(
                    pk.at[kind, yidx[d] * HG + g], into.at[g, rows],
                    ysend.at[kind, g, d - 1], yrecv.at[kind, g, d - 1], s, ycol[d],
                )
                c.start()
                group.append(c)
                sends.append(c)
            into[g, rows, :] = pk[kind, y * HG + g]
            copies.append(group)
        return copies

    def block(ref, g, index):
        return ref.at[g, pl.ds(pl.multiple_of(index * 256, 256), 256)]

    def spread(kind, ref, copies):
        out_copies = []
        for g in range(HG):
            for c in copies[g]:
                c.wait_recv()
            a = remote(block(ref, g, w), block(ref, g, w), wsend.at[kind, g, 0], wrecv.at[kind, g, 0], s, far)
            b = remote(block(ref, g, w), block(ref, g, w), wsend.at[kind, g, 1], wrecv.at[kind, g, 1], s, core)
            a.start()
            b.start()
            sends.extend((a, b))
            out_copies.append((a, b))
        return out_copies

    def relay(kind, ref, copies, g):
        a, b = copies[g]
        a.wait_recv()
        c = remote(block(ref, g, w_far), block(ref, g, w_far), wsend.at[kind, g, 2], wrecv.at[kind, g, 2], s, core)
        c.start()
        sends.append(c)
        b.wait_recv()
        return c

    ky = project(0, wk, loads[0], kb, (w * NY + y) * CL)
    qy = project(1, wq, loads[1], qb, y * CL, masked=True)
    kw = spread(0, kb, ky)
    vy = project(2, wv, loads[2], vb, (w * NY + y) * CL)

    rcopies = []
    for g in range(HG):
        c = relay(0, kb, kw, g)
        for q in qy[g]:
            q.wait_recv()
        c.wait_recv()
        for j in range(4):
            part[g, :, j * 256:(j + 1) * 256] = dot(qb[g], kb[g, j * 256:(j + 1) * 256, :], ((1,), (1,)))
        group = []
        for d in range(1, NS):
            c = remote(
                part.at[g, pl.ds(pl.multiple_of(sidx[d] * 32, 32), 32)], rs.at[g, d - 1],
                rsend.at[g, d - 1], rrecv.at[g, d - 1], sidx[d], col,
            )
            c.start()
            group.append(c)
            sends.append(c)
        rcopies.append(group)

    vw = spread(1, vb, vy)
    pcopies = []
    mine = pl.ds(pl.multiple_of(s * 32, 32), 32)
    for g in range(HG):
        for c in rcopies[g]:
            c.wait_recv()
        total = part[g, mine, :]
        for d in range(NS - 1):
            total = total + rs[g, d]
        total = total * (1.0 / 64.0)
        e = jnp.exp(total - jnp.max(total, axis=-1, keepdims=True))
        pw[g, mine, :] = (e / jnp.sum(e, axis=-1, keepdims=True)).astype(BF)
        group = []
        for d in range(1, NS):
            c = remote(pw.at[g, mine], pw.at[g, mine], psend.at[g, d - 1], precv.at[g, d - 1], sidx[d], col)
            c.start()
            group.append(c)
            sends.append(c)
        pcopies.append(group)
    vd = [relay(1, vb, vw, g) for g in range(HG)]

    mcopies = []
    for g in range(HG):
        vd[g].wait_recv()
        for c in pcopies[g]:
            c.wait_recv()
        mxs[g] = dot(pw[g], vb[g]).astype(BF)
        for d in range(1, NY):
            c = remote(
                mxs.at[g, pl.ds(pl.multiple_of(yidx[d] * CL, CL), CL)], mxr.at[y * HG + g],
                msend.at[g, d - 1], mrecv.at[g, d - 1], s, ycol[d],
            )
            c.start()
            mcopies.append(c)
            sends.append(c)
        mxr[y * HG + g] = mxs[g, pl.ds(pl.multiple_of(y * CL, CL), CL), :]
    for c in mcopies:
        c.wait_recv()
    for p in range(RL // 2):
        for hp in range(H // 2):
            a = mxr[2 * hp, :, p * 128:(p + 1) * 128].astype(F32)
            b = mxr[2 * hp + 1, :, p * 128:(p + 1) * 128].astype(F32)
            first, second = pair_lanes(a, b)
            xn[2 * p * CL:(2 * p + 1) * CL, hp * 128:(hp + 1) * 128] = first.astype(BF)
            xn[(2 * p + 1) * CL:(2 * p + 2) * CL, hp * 128:(hp + 1) * 128] = second.astype(BF)
    loads[3].wait()
    acc[...] = x[...].astype(F32) + dot(xn[...], wo[...])
    ccopies = []
    for t in range(NS):
        rows = [acc[r * CL + t * RL:r * CL + (t + 1) * RL, :] for r in range(RL)]
        cs[t] = jnp.concatenate(rows, axis=0).astype(BF)
    for d in range(1, NS):
        c = remote(cs.at[sidx[d]], out.at[s], csend.at[d - 1], crecv.at[d - 1], sidx[d], col)
        c.start()
        ccopies.append(c)
        sends.append(c)
    out[s] = cs[s]
    for c in ccopies:
        c.wait_recv()
    for c in sends:
        c.wait_send()


def col_kernel(
    mask, x, gc, gf, wq_h, wk_h, wv_h, wo_h, up_h, dn_h, out,
    wq, wk, wv, wo, up, dn, xf, xo, cin, qc, kc, vc, hb, facc, cs, cr,
    wsem, csend, crecv,
):
    s, y, w = place()
    col = y * NW + w
    sidx = [None] + [lax.rem(s + d, NS) for d in range(1, NS)]
    loads = []
    for i, (h, v) in enumerate(((wq_h, wq), (wk_h, wk), (wv_h, wv), (wo_h, wo), (up_h, up), (dn_h, dn))):
        loads.append(pltpu.make_async_copy(h, v, wsem.at[i]))
        loads[-1].start()
    greet([(d, col) for d in sidx[1:]])

    for j in range(D // 128):
        xf[j] = x[:, j * 128:(j + 1) * 128].astype(F32)
    for c in range(RL):
        xc = jnp.concatenate([xf[j, pl.ds(c, 64, stride=RL), :] for j in range(D // 128)], axis=1)
        xo[c * 64:(c + 1) * 64, :] = xc
        cin[c * 64:(c + 1) * 64, :] = norm(xc, gc[...].astype(F32)).astype(BF)
    for load, weight, into in ((loads[0], wq, qc), (loads[1], wk, kc), (loads[2], wv, vc)):
        load.wait()
        into[...] = dot(cin[...], weight[...]).astype(BF)

    live = mask[...] > 0
    lane = lax.broadcasted_iota(jnp.int32, (1, 256), 1)
    pick = [((lane >= h * 64) & (lane < (h + 1) * 64)).astype(F32) for h in range(4)]

    @pl.loop(0, RL)
    def _(c):
        rows = pl.ds(pl.multiple_of(c * 64, 64), 64)
        for g in range(3):
            lanes = slice(g * 256, (g + 1) * 256)
            q = qc[rows, lanes]
            qe = jnp.concatenate([q * pick[h].astype(BF) for h in range(4)], axis=0)
            st = dot(kc[rows, lanes], qe, ((1,), (1,))) * 0.125
            st = jnp.where(live, st, -1e30)
            e = jnp.exp(st - jnp.max(st, axis=0, keepdims=True))
            p = (e / jnp.sum(e, axis=0, keepdims=True)).astype(BF)
            res = dot(p, vc[rows, lanes], ((0,), (0,)))
            mixed = res[0:64] * pick[0]
            for h in range(1, 4):
                mixed = mixed + res[h * 64:(h + 1) * 64] * pick[h]
            cin[rows, lanes] = mixed.astype(BF)

    loads[3].wait()
    after = (xo[...] + dot(cin[...], wo[...])).astype(BF).astype(F32)
    facc[...] = after
    cin[...] = norm(after, gf[...].astype(F32)).astype(BF)
    loads[4].wait()
    loads[5].wait()

    @pl.loop(0, FF // D)
    def _(n):
        part = pl.ds(pl.multiple_of(n * D, D), D)
        h = dot(cin[...], up[:, part])
        hb[...] = (0.5 * h * (1.0 + lax.erf(h * 0.7071067811865476))).astype(BF)
        facc[...] += dot(hb[...], dn[part, :])

    for j in range(D // 128):
        lanes = slice(j * 128, (j + 1) * 128)
        for c in range(RL):
            xf[j, pl.ds(c, 64, stride=RL), :] = facc[c * 64:(c + 1) * 64, lanes]
        for t in range(NS):
            cs[t, :, lanes] = xf[j, t * 64:(t + 1) * 64, :].astype(BF)
    copies = []
    for d in range(1, NS):
        c = remote(cs.at[sidx[d]], cr.at[s], csend.at[d - 1], crecv.at[d - 1], sidx[d], col)
        c.start()
        copies.append(c)
    cr[s] = cs[s]
    for c in copies:
        c.wait_recv()
    for m in range(NS // 2):
        a = cr[2 * m].astype(F32)
        b = cr[2 * m + 1].astype(F32)
        for r in range(RL):
            both = jnp.concatenate([a[r * 8:(r + 1) * 8], b[r * 8:(r + 1) * 8]], axis=0)
            out[r * CL + m * 16:r * CL + (m + 1) * 16, :] = both.astype(BF)
    for c in copies:
        c.wait_send()


def vmem():
    return pl.BlockSpec(memory_space=pltpu.VMEM)


def hbm():
    return pl.BlockSpec(memory_space=pl.ANY)


def dma(*shape):
    return pltpu.SemaphoreType.DMA(shape)


def local(
    stream, row_mask, gain_row, row_query, row_key, row_value, row_output,
    gain_column, column_query, column_key, column_value, column_output,
    gain_feed, up_weight, down_weight,
):
    x = stream.reshape(T, D)
    weight = pltpu.VMEM((D, D), BF)
    moved = pl.pallas_call(
        row_kernel,
        out_shape=jax.ShapeDtypeStruct((NS, 64, D), BF),
        in_specs=[pl.BlockSpec(memory_space=pltpu.SMEM), vmem(), vmem()] + [hbm()] * 4,
        out_specs=vmem(),
        scratch_shapes=[
            weight, weight, weight, weight,
            pltpu.VMEM((T, D), BF),
            pltpu.VMEM((T, D), F32),
            pltpu.VMEM((3, H, CL, 512), BF),
            pltpu.VMEM((HG, 256, 512), BF),
            pltpu.VMEM((HG, 1024, 512), BF),
            pltpu.VMEM((HG, 1024, 512), BF),
            pltpu.VMEM((HG, 256, 1024), F32),
            pltpu.VMEM((HG, NS - 1, 32, 1024), F32),
            pltpu.VMEM((HG, 256, 1024), BF),
            pltpu.VMEM((HG, 256, 512), BF),
            pltpu.VMEM((H, CL, 512), BF),
            pltpu.VMEM((NS, 64, D), BF),
            dma(4),
            dma(3, HG, NY - 1), dma(3, HG, NY - 1),
            dma(2, HG, 3), dma(2, HG, 3),
            dma(HG, NS - 1), dma(HG, NS - 1),
            dma(HG, NS - 1), dma(HG, NS - 1),
            dma(HG, NY - 1), dma(HG, NY - 1),
            dma(NS - 1), dma(NS - 1),
        ],
        compiler_params=pltpu.CompilerParams(
            collective_id=0, has_side_effects=True, vmem_limit_bytes=VMEM_LIMIT
        ),
        name="row_attention",
    )(row_mask, x, gain_row.reshape(1, D), row_query, row_key, row_value, row_output)
    out = pl.pallas_call(
        col_kernel,
        out_shape=jax.ShapeDtypeStruct((T, D), BF),
        in_specs=[vmem()] * 4 + [hbm()] * 6,
        out_specs=vmem(),
        scratch_shapes=[
            weight, weight, weight, weight,
            pltpu.VMEM((D, FF), BF),
            pltpu.VMEM((FF, D), BF),
            pltpu.VMEM((D // 128, T, 128), F32),
            pltpu.VMEM((T, D), F32),
            pltpu.VMEM((T, D), BF),
            pltpu.VMEM((T, D), BF),
            pltpu.VMEM((T, D), BF),
            pltpu.VMEM((T, D), BF),
            pltpu.VMEM((T, D), BF),
            pltpu.VMEM((T, D), F32),
            pltpu.VMEM((NS, 64, D), BF),
            pltpu.VMEM((NS, 64, D), BF),
            dma(6),
            dma(NS - 1), dma(NS - 1),
        ],
        compiler_params=pltpu.CompilerParams(
            collective_id=1, has_side_effects=True, vmem_limit_bytes=VMEM_LIMIT
        ),
        name="column_and_feed",
    )(
        row_mask.reshape(64, 1), moved.reshape(T, D), gain_column.reshape(1, D), gain_feed.reshape(1, D),
        column_query, column_key, column_value, column_output, up_weight, down_weight,
    )
    return out.reshape(RL, CL, D)


def solution(mesh):
    return jax.shard_map(
        local,
        mesh=mesh,
        in_specs=(P("seq", "col", None),) + (P(),) * 14,
        out_specs=P("seq", "col", None),
        check_vma=False,
    )
```

```python
import jax
import jax.numpy as jnp
from jax import lax
from jax.experimental import pallas as pl
from jax.experimental.pallas import tpu as pltpu
from jax.sharding import PartitionSpec as P

D = 768
H = 12
DH = 64
FF = 3072
RL = 8
CL = 64
T = RL * CL
NS = 8
NZ = 4
NY = 4
NW = 4
HG = H // NY
BF = jnp.bfloat16
F32 = jnp.float32
MESH = pl.DeviceIdType.MESH
VMEM_LIMIT = 60 * 1024 * 1024


def norm(wide, gain):
    center = wide - jnp.mean(wide, axis=-1, keepdims=True)
    spread = jnp.mean(center * center, axis=-1, keepdims=True)
    return center * lax.rsqrt(spread + 1e-05) * gain


def dot(a, b, dims=((1,), (0,))):
    return lax.dot_general(a, b, (dims, ((), ())), preferred_element_type=F32)


def chunk(index, size):
    return pl.ds(pl.multiple_of(index * size, size), size)


class Load:
    def __init__(self, src, dst, sem):
        self.copy = pltpu.make_async_copy(src, dst, sem)
        self.copy.start()
        self.done = False

    def wait(self):
        if not self.done:
            self.copy.wait()
        self.done = True


class Push:
    def __init__(self, log, src, dst, sems, index, to):
        send, recv = sems
        self.copy = pltpu.make_async_remote_copy(
            src_ref=src, dst_ref=dst, send_sem=send.at[index], recv_sem=recv.at[index],
            device_id=to, device_id_type=MESH,
        )
        self.copy.start()
        self.got = self.left = False
        log.append(self)

    def recv(self):
        if not self.got:
            self.copy.wait_recv()
        self.got = True

    def sent(self):
        if not self.left:
            self.copy.wait_send()
        self.left = True


def finish(log, loads):
    for load in loads:
        load.wait()
    for push in log:
        push.recv()
    for push in log:
        push.sent()


def greet(peers):
    barrier = pltpu.get_barrier_semaphore()
    for peer in peers:
        pl.semaphore_signal(barrier, inc=1, device_id=peer, device_id_type=MESH)
    pl.semaphore_wait(barrier, len(peers))


def pair_lanes(a, b):
    low = lax.broadcasted_iota(jnp.int32, a.shape, 1) < DH
    return jnp.where(low, a, pltpu.roll(b, DH, 1)), jnp.where(low, pltpu.roll(a, DH, 1), b)


def layer_kernel(
    mask, x, gr, gc, gf, rq_h, rk_h, rv_h, ro_h, cq_h, ck_h, cv_h, co_h, up_h, dn_h, out,
    wrk, wrq, wrv, wro, wcq, wck, wcv, wco, up, dn,
    xn, acc, pk, qb, kb, vb, part, pb, rs, th, xs, xr, pw, mxs, mxr, cs, ci,
    xf, xo, cin, qc, kc, vc, hb, facc, cr, bias,
    lsem, ys, yr, fs, fr, zs, zr, hs, hr, as_, ar, ms, mr, cs_s, cs_r, os_, or_,
):
    s = lax.axis_index("seq")
    col = lax.axis_index("col")
    y, w = lax.div(col, NW), lax.rem(col, NW)
    xl, z = lax.div(s, NZ), lax.rem(s, NZ)
    yidx = [lax.rem(y + d, NY) for d in range(NY)]
    ydev = [(s, yidx[d] * NW + w) for d in range(NY)]
    zidx = [lax.rem(z + d, NZ) for d in range(NZ)]
    zdev = [(xl * NZ + zidx[d], col) for d in range(NZ)]
    xdev = ((1 - xl) * NZ + z, col)
    sidx = [lax.rem(s + d, NS) for d in range(NS)]
    sdev = [(sidx[d], col) for d in range(NS)]
    w_far = lax.rem(w + 2, NW)
    far = (s, y * NW + w_far)
    core = (s, y * NW + w + 1 - 2 * lax.rem(w, 2))

    pairs = (
        (rk_h, wrk), (rq_h, wrq), (rv_h, wrv), (ro_h, wro), (cq_h, wcq), (ck_h, wck), (cv_h, wcv),
        (co_h, wco), (up_h, up), (dn_h, dn),
    )
    loads = [Load(h, v, lsem.at[i]) for i, (h, v) in enumerate(pairs)]
    greet(ydev[1:] + [far, core] + sdev[1:])
    log = []

    def gain(ref):
        return ref[...].astype(F32).reshape(1, D)

    xn[...] = norm(x[...].astype(F32), gain(gr)).astype(BF)

    def project(kind, weight, load, into, base, masked=False):
        load.wait()
        acc[...] = dot(xn[...], weight[...])
        for p in range(RL // 2):
            for hp in range(H // 2):
                a = acc[2 * p * CL:(2 * p + 1) * CL, hp * 128:(hp + 1) * 128]
                b = acc[(2 * p + 1) * CL:(2 * p + 2) * CL, hp * 128:(hp + 1) * 128]
                if masked:
                    a = a * mask[s * RL + 2 * p].astype(F32)
                    b = b * mask[s * RL + 2 * p + 1].astype(F32)
                first, second = pair_lanes(a, b)
                pk[kind, 2 * hp, :, p * 128:(p + 1) * 128] = first.astype(BF)
                pk[kind, 2 * hp + 1, :, p * 128:(p + 1) * 128] = second.astype(BF)
        rows = chunk(base, CL)
        pushes = []
        for g in range(HG):
            pushes.append([
                Push(log, pk.at[kind, yidx[d] * HG + g], into.at[g, rows], (ys, yr), (kind, g, d - 1), ydev[d])
                for d in (2, 1, 3)
            ])
            into[g, rows, :] = pk[kind, y * HG + g]
        return pushes

    def spread(kind, ref, pushes, g):
        for p in pushes[g]:
            p.recv()
        block = ref.at[g, chunk(w, 256)]
        return (
            Push(log, block, block, (fs, fr), (kind, g, 0), far),
            Push(log, block, block, (fs, fr), (kind, g, 1), core),
        )

    def relay(kind, ref, pushes, g):
        pushes[0].recv()
        block = ref.at[g, chunk(w_far, 256)]
        last = Push(log, block, block, (fs, fr), (kind, g, 2), core)
        pushes[1].recv()
        return last

    def logits(g, last):
        for p in qy[g]:
            p.recv()
        last.recv()
        for j in range(4):
            part[g, :, j * 256:(j + 1) * 256] = dot(qb[g], kb[g, j * 256:(j + 1) * 256, :], ((1,), (1,)))
        shifted = part[g] - jnp.max(part[g], axis=-1, keepdims=True)
        part[g] = shifted
        pb[g] = shifted.astype(BF)
        return [
            Push(log, pb.at[g, chunk(zidx[d], 64)], rs.at[g, d - 1], (zs, zr), (g, d - 1), zdev[d]) for d in (2, 1, 3)
        ]

    def over_z(g, pushes):
        for p in pushes:
            p.recv()

        def half(index):
            total = part[g, chunk(z * 2 + index, 32), :]
            for d in range(NZ - 1):
                total = total + rs[g, d, chunk(index, 32), :].astype(F32)
            return total

        xs[g] = half(1 - xl)
        push = Push(log, xs.at[g], xr.at[g], (hs, hr), (g,), xdev)
        th[g] = half(xl)
        return push

    def soften(g, push):
        push.recv()
        total = (th[g] + xr[g]) * (1.0 / 64.0)
        e = jnp.exp(total - jnp.max(total, axis=-1, keepdims=True))
        rows = chunk(z * 2 + xl, 32)
        pw[g, rows, :] = (e / jnp.sum(e, axis=-1, keepdims=True)).astype(BF)
        block = pw.at[g, rows]
        return [Push(log, block, block, (as_, ar), (g, 0), xdev)] + [
            Push(log, block, block, (as_, ar), (g, d), zdev[d]) for d in (2, 1, 3)
        ]

    def onward(g, pushes):
        pushes[0].recv()
        block = pw.at[g, chunk(z * 2 + 1 - xl, 32)]
        return pushes + [Push(log, block, block, (as_, ar), (g, 3 + d), zdev[d]) for d in (2, 1, 3)]

    def mix(g, last, pushes):
        last.recv()
        for p in pushes:
            p.recv()
        mxs[g] = dot(pw[g], vb[g]).astype(BF)
        got = [
            Push(log, mxs.at[g, chunk(yidx[d], CL)], mxr.at[y * HG + g], (ms, mr), (g, d - 1), ydev[d])
            for d in (2, 1, 3)
        ]
        mxr[y * HG + g] = mxs[g, chunk(y, CL), :]
        return got

    own = w * NY + y
    ky = project(0, wrk, loads[0], kb, own)
    qy = project(1, wrq, loads[1], qb, y, masked=True)
    k0 = spread(0, kb, ky, 0)
    vy = project(2, wrv, loads[2], vb, own)
    k1 = spread(0, kb, ky, 1)
    k2 = spread(0, kb, ky, 2)
    k0 = relay(0, kb, k0, 0)
    z0 = logits(0, k0)
    k1 = relay(0, kb, k1, 1)
    z1 = logits(1, k1)
    x0 = over_z(0, z0)
    k2 = relay(0, kb, k2, 2)
    z2 = logits(2, k2)
    p0 = soften(0, x0)
    x1 = over_z(1, z1)
    v0 = spread(1, vb, vy, 0)
    p0 = onward(0, p0)
    p1 = soften(1, x1)
    v1 = spread(1, vb, vy, 1)
    x2 = over_z(2, z2)
    p1 = onward(1, p1)
    v2 = spread(1, vb, vy, 2)
    p2 = soften(2, x2)
    v0 = relay(1, vb, v0, 0)
    p2 = onward(2, p2)
    v1 = relay(1, vb, v1, 1)
    v2 = relay(1, vb, v2, 2)
    m = mix(0, v0, p0)
    m = m + mix(1, v1, p1)
    m = m + mix(2, v2, p2)
    for p in m:
        p.recv()
    for p in range(RL // 2):
        for hp in range(H // 2):
            a = mxr[2 * hp, :, p * 128:(p + 1) * 128].astype(F32)
            b = mxr[2 * hp + 1, :, p * 128:(p + 1) * 128].astype(F32)
            first, second = pair_lanes(a, b)
            xn[2 * p * CL:(2 * p + 1) * CL, hp * 128:(hp + 1) * 128] = first.astype(BF)
            xn[(2 * p + 1) * CL:(2 * p + 2) * CL, hp * 128:(hp + 1) * 128] = second.astype(BF)
    loads[3].wait()
    acc[...] = x[...].astype(F32) + dot(xn[...], wro[...])
    for t in range(NS):
        rows = [acc[r * CL + t * RL:r * CL + (t + 1) * RL, :] for r in range(RL)]
        cs[t] = jnp.concatenate(rows, axis=0).astype(BF)
    c_in = [Push(log, cs.at[sidx[d]], ci.at[s], (cs_s, cs_r), (d - 1,), sdev[d]) for d in range(1, NS)]
    ci[s] = cs[s]

    row = lax.broadcasted_iota(jnp.int32, (8, 128), 0)
    for t in range(NS):
        tile = jnp.zeros((8, 128), F32)
        for k in range(8):
            tile = jnp.where(row == k, mask[t * 8 + k].astype(F32), tile)
        bias[t * 8:(t + 1) * 8, :] = tile
    for p in c_in:
        p.recv()

    for j in range(D // 128):
        xf[j] = ci[:, :, j * 128:(j + 1) * 128].astype(F32).reshape(T, 128)
    for c in range(RL):
        xc = jnp.concatenate([xf[j, pl.ds(c, 64, stride=RL), :] for j in range(D // 128)], axis=1)
        xo[c * 64:(c + 1) * 64, :] = xc
        cin[c * 64:(c + 1) * 64, :] = norm(xc, gain(gc)).astype(BF)
    for load, weight, into in ((loads[4], wcq, qc), (loads[5], wck, kc), (loads[6], wcv, vc)):
        load.wait()
        into[...] = dot(cin[...], weight[...]).astype(BF)

    live = jnp.concatenate([bias[...], bias[...]], axis=1) > 0.5
    lane = lax.broadcasted_iota(jnp.int32, (1, 256), 1)
    pick = [((lane >= h * 64) & (lane < (h + 1) * 64)).astype(F32) for h in range(4)]

    @pl.loop(0, RL)
    def _(c):
        rows = chunk(c, 64)
        for g in range(3):
            lanes = slice(g * 256, (g + 1) * 256)
            q = qc[rows, lanes]
            qe = jnp.concatenate([q * pick[h].astype(BF) for h in range(4)], axis=0)
            st = dot(kc[rows, lanes], qe, ((1,), (1,))) * 0.125
            st = jnp.where(live, st, -1e30)
            e = jnp.exp(st - jnp.max(st, axis=0, keepdims=True))
            p = (e / jnp.sum(e, axis=0, keepdims=True)).astype(BF)
            res = dot(p, vc[rows, lanes], ((0,), (0,)))
            mixed = res[0:64] * pick[0]
            for h in range(1, 4):
                mixed = mixed + res[h * 64:(h + 1) * 64] * pick[h]
            cin[rows, lanes] = mixed.astype(BF)

    loads[7].wait()
    after = (xo[...] + dot(cin[...], wco[...])).astype(BF).astype(F32)
    facc[...] = after
    cin[...] = norm(after, gain(gf)).astype(BF)
    loads[8].wait()
    loads[9].wait()

    @pl.loop(0, FF // D)
    def _(n):
        part_n = chunk(n, D)
        h = dot(cin[...], up[:, part_n])
        hb[...] = (0.5 * h * (1.0 + lax.erf(h * 0.7071067811865476))).astype(BF)
        facc[...] += dot(hb[...], dn[part_n, :])
    for p in c_in:
        p.sent()
    for j in range(D // 128):
        lanes = slice(j * 128, (j + 1) * 128)
        for c in range(RL):
            xf[j, pl.ds(c, 64, stride=RL), :] = facc[c * 64:(c + 1) * 64, lanes]
        for t in range(NS):
            cs[t, :, lanes] = xf[j, t * 64:(t + 1) * 64, :].astype(BF)
    back = [Push(log, cs.at[sidx[d]], cr.at[s], (os_, or_), (d - 1,), sdev[d]) for d in range(1, NS)]
    cr[s] = cs[s]
    for p in back:
        p.recv()
    for m in range(NS // 2):
        a = cr[2 * m].astype(F32)
        b = cr[2 * m + 1].astype(F32)
        for r in range(RL):
            both = jnp.concatenate([a[r * 8:(r + 1) * 8], b[r * 8:(r + 1) * 8]], axis=0)
            out[r * CL + m * 16:r * CL + (m + 1) * 16, :] = both.astype(BF)
    finish(log, loads)


def vmem():
    return pl.BlockSpec(memory_space=pltpu.VMEM)


def hbm():
    return pl.BlockSpec(memory_space=pl.ANY)


def pairs_of(*shape):
    return [pltpu.SemaphoreType.DMA(shape)] * 2


def local(
    stream, row_mask, gain_row, row_query, row_key, row_value, row_output,
    gain_column, column_query, column_key, column_value, column_output,
    gain_feed, up_weight, down_weight,
):
    def bf(*shape):
        return pltpu.VMEM(shape, BF)

    def f32(*shape):
        return pltpu.VMEM(shape, F32)

    out = pl.pallas_call(
        layer_kernel,
        out_shape=jax.ShapeDtypeStruct((T, D), BF),
        in_specs=[pl.BlockSpec(memory_space=pltpu.SMEM)] + [vmem()] * 4 + [hbm()] * 10,
        out_specs=vmem(),
        scratch_shapes=[bf(D, D)] * 8 + [
            bf(D, FF), bf(FF, D),
            bf(T, D), f32(T, D), bf(3, H, CL, 512),
            bf(HG, 256, 512), bf(HG, 1024, 512), bf(HG, 1024, 512),
            f32(HG, 256, 1024), bf(HG, 256, 1024), bf(HG, NZ - 1, 64, 1024),
            f32(HG, 32, 1024), f32(HG, 32, 1024), f32(HG, 32, 1024),
            bf(HG, 256, 1024), bf(HG, 256, 512), bf(H, CL, 512),
            bf(NS, 64, D), bf(NS, 64, D),
            f32(D // 128, T, 128), f32(T, D), bf(T, D), bf(T, D), bf(T, D), bf(T, D), bf(T, D),
            f32(T, D), bf(NS, 64, D), f32(64, 128),
            pltpu.SemaphoreType.DMA((10,)),
        ] + pairs_of(3, HG, NY - 1) + pairs_of(2, HG, 3) + pairs_of(HG, NZ - 1) + pairs_of(HG)
        + pairs_of(HG, 7) + pairs_of(HG, NY - 1) + pairs_of(NS - 1) + pairs_of(NS - 1),
        compiler_params=pltpu.CompilerParams(
            collective_id=0, has_side_effects=True, vmem_limit_bytes=VMEM_LIMIT
        ),
        name="layer",
    )(
        row_mask, stream.reshape(T, D), gain_row, gain_column, gain_feed,
        row_query, row_key, row_value, row_output,
        column_query, column_key, column_value, column_output, up_weight, down_weight,
    )
    return out.reshape(RL, CL, D)


def solution(mesh):
    return jax.shard_map(
        local,
        mesh=mesh,
        in_specs=(P("seq", "col", None),) + (P(),) * 14,
        out_specs=P("seq", "col", None),
        check_vma=False,
    )
```

```python
import jax
import jax.numpy as jnp
from jax import lax
from jax.experimental import pallas as pl
from jax.experimental.pallas import tpu as pltpu
from jax.sharding import PartitionSpec as P

D = 768
H = 12
DH = 64
FF = 3072
RL = 8
CL = 64
T = RL * CL
NS = 8
NZ = 4
NY = 4
NW = 4
HG = H // NY
BF = jnp.bfloat16
F32 = jnp.float32
MESH = pl.DeviceIdType.MESH
VMEM_LIMIT = 60 * 1024 * 1024


def norm(wide, gain):
    center = wide - jnp.mean(wide, axis=-1, keepdims=True)
    spread = jnp.mean(center * center, axis=-1, keepdims=True)
    return center * lax.rsqrt(spread + 1e-05) * gain


def dot(a, b, dims=((1,), (0,))):
    return lax.dot_general(a, b, (dims, ((), ())), preferred_element_type=F32)


def chunk(index, size):
    return pl.ds(pl.multiple_of(index * size, size), size)


class Load:
    def __init__(self, src, dst, sem):
        self.copy = pltpu.make_async_copy(src, dst, sem)
        self.copy.start()
        self.done = False

    def wait(self):
        if not self.done:
            self.copy.wait()
        self.done = True


class Push:
    def __init__(self, log, src, dst, sems, index, to):
        send, recv = sems
        self.copy = pltpu.make_async_remote_copy(
            src_ref=src, dst_ref=dst, send_sem=send.at[index], recv_sem=recv.at[index],
            device_id=to, device_id_type=MESH,
        )
        self.copy.start()
        self.got = self.left = False
        log.append(self)

    def recv(self):
        if not self.got:
            self.copy.wait_recv()
        self.got = True

    def sent(self):
        if not self.left:
            self.copy.wait_send()
        self.left = True


def finish(log, loads):
    for load in loads:
        load.wait()
    for push in log:
        push.recv()
    for push in log:
        push.sent()


def pair_lanes(a, b):
    low = lax.broadcasted_iota(jnp.int32, a.shape, 1) < DH
    return jnp.where(low, a, pltpu.roll(b, DH, 1)), jnp.where(low, pltpu.roll(a, DH, 1), b)


def layer_kernel(
    mask, x, gr, gc, gf, rq_h, rk_h, rv_h, ro_h, cq_h, ck_h, cv_h, co_h, up_h, dn_h, out,
    wrk, wrq, wrv, wro, wcq, wck, wcv, wco, up, dn,
    xn, acc, pk, qb, kb, vb, part, pb, rs, th, xs, xr, pw, mxs, mxr, cs, ci,
    xf, xo, cin, qc, kc, vc, hb, facc, co, cr, bias,
    lsem, ys, yr, fs, fr, zs, zr, hs, hr, as_, ar, ms, mr, cs_s, cs_r, os_, or_,
):
    s = lax.axis_index("seq")
    col = lax.axis_index("col")
    y, w = lax.div(col, NW), lax.rem(col, NW)
    xl, z = lax.div(s, NZ), lax.rem(s, NZ)
    yidx = [lax.rem(y + d, NY) for d in range(NY)]
    ydev = [(s, yidx[d] * NW + w) for d in range(NY)]
    zidx = [lax.rem(z + d, NZ) for d in range(NZ)]
    zdev = [(xl * NZ + zidx[d], col) for d in range(NZ)]
    xdev = ((1 - xl) * NZ + z, col)
    sidx = [lax.rem(s + d, NS) for d in range(NS)]
    sdev = [(sidx[d], col) for d in range(NS)]
    w_far = lax.rem(w + 2, NW)
    far = (s, y * NW + w_far)
    core = (s, y * NW + w + 1 - 2 * lax.rem(w, 2))

    pairs = (
        (rk_h, wrk), (rq_h, wrq), (rv_h, wrv), (ro_h, wro), (cq_h, wcq), (ck_h, wck), (cv_h, wcv),
        (co_h, wco), (up_h, up), (dn_h, dn),
    )
    loads = [Load(h, v, lsem.at[i]) for i, (h, v) in enumerate(pairs)]
    barrier = pltpu.get_barrier_semaphore()
    peers = ydev[1:] + [far, core] + sdev[1:]
    for peer in peers:
        pl.semaphore_signal(barrier, inc=1, device_id=peer, device_id_type=MESH)
    log = []

    def gain(ref):
        return ref[...].astype(F32).reshape(1, D)

    xn[...] = norm(x[...].astype(F32), gain(gr)).astype(BF)

    def project(kind, weight, load, masked=False):
        load.wait()
        acc[...] = dot(xn[...], weight[...])
        for p in range(RL // 2):
            for hp in range(H // 2):
                a = acc[2 * p * CL:(2 * p + 1) * CL, hp * 128:(hp + 1) * 128]
                b = acc[(2 * p + 1) * CL:(2 * p + 2) * CL, hp * 128:(hp + 1) * 128]
                if masked:
                    a = a * mask[s * RL + 2 * p].astype(F32)
                    b = b * mask[s * RL + 2 * p + 1].astype(F32)
                first, second = pair_lanes(a, b)
                pk[kind, 2 * hp, :, p * 128:(p + 1) * 128] = first.astype(BF)
                pk[kind, 2 * hp + 1, :, p * 128:(p + 1) * 128] = second.astype(BF)

    def over_y(kind, into, base, g):
        rows = chunk(base, CL)
        pushes = [
            Push(log, pk.at[kind, yidx[d] * HG + g], into.at[g, rows], (ys, yr), (kind, g, d - 1), ydev[d])
            for d in (2, 1, 3)
        ]
        into[g, rows, :] = pk[kind, y * HG + g]
        return pushes

    def spread(kind, ref, pushes, g):
        for p in pushes[g]:
            p.recv()
        block = ref.at[g, chunk(w, 256)]
        return (
            Push(log, block, block, (fs, fr), (kind, g, 0), far),
            Push(log, block, block, (fs, fr), (kind, g, 1), core),
        )

    def relay(kind, ref, pushes, g):
        pushes[0].recv()
        block = ref.at[g, chunk(w_far, 256)]
        last = Push(log, block, block, (fs, fr), (kind, g, 2), core)
        pushes[1].recv()
        return last

    def logits(g, last):
        for p in qy[g]:
            p.recv()
        last.recv()
        for j in range(4):
            part[g, :, j * 256:(j + 1) * 256] = dot(qb[g], kb[g, j * 256:(j + 1) * 256, :], ((1,), (1,)))
        shifted = part[g] - jnp.max(part[g], axis=-1, keepdims=True)
        part[g] = shifted
        pb[g] = shifted.astype(BF)
        return [
            Push(log, pb.at[g, chunk(zidx[d], 64)], rs.at[g, d - 1], (zs, zr), (g, d - 1), zdev[d]) for d in (2, 1, 3)
        ]

    def over_z(g, pushes):
        for p in pushes:
            p.recv()

        def half(index):
            total = part[g, chunk(z * 2 + index, 32), :]
            for d in range(NZ - 1):
                total = total + rs[g, d, chunk(index, 32), :].astype(F32)
            return total

        xs[g] = half(1 - xl)
        push = Push(log, xs.at[g], xr.at[g], (hs, hr), (g,), xdev)
        th[g] = half(xl)
        return push

    def soften(g, push):
        push.recv()
        total = (th[g] + xr[g]) * (1.0 / 64.0)
        e = jnp.exp(total - jnp.max(total, axis=-1, keepdims=True))
        rows = chunk(z * 2 + xl, 32)
        pw[g, rows, :] = (e / jnp.sum(e, axis=-1, keepdims=True)).astype(BF)
        block = pw.at[g, rows]
        return [Push(log, block, block, (as_, ar), (g, 0), xdev)] + [
            Push(log, block, block, (as_, ar), (g, d), zdev[d]) for d in (2, 1, 3)
        ]

    def onward(g, pushes):
        pushes[0].recv()
        block = pw.at[g, chunk(z * 2 + 1 - xl, 32)]
        return pushes + [Push(log, block, block, (as_, ar), (g, 3 + d), zdev[d]) for d in (2, 1, 3)]

    def mix(g, last, pushes):
        last.recv()
        for p in pushes:
            p.recv()
        mxs[g] = dot(pw[g], vb[g]).astype(BF)
        got = [
            Push(log, mxs.at[g, chunk(yidx[d], CL)], mxr.at[y * HG + g], (ms, mr), (g, d - 1), ydev[d])
            for d in (2, 1, 3)
        ]
        mxr[y * HG + g] = mxs[g, chunk(y, CL), :]
        return got

    own = w * NY + y
    ky, qy, vy = [None] * HG, [None] * HG, [None] * HG
    project(0, wrk, loads[0])
    pl.semaphore_wait(barrier, len(peers))
    ky[0] = over_y(0, kb, own, 0)
    project(1, wrq, loads[1], masked=True)
    qy[0] = over_y(1, qb, y, 0)
    for g in range(1, HG):
        ky[g] = over_y(0, kb, own, g)
        qy[g] = over_y(1, qb, y, g)
    k0 = spread(0, kb, ky, 0)
    project(2, wrv, loads[2])
    for g in range(HG):
        vy[g] = over_y(2, vb, own, g)
    k1 = spread(0, kb, ky, 1)
    k0 = relay(0, kb, k0, 0)
    z0 = logits(0, k0)
    k2 = spread(0, kb, ky, 2)
    k1 = relay(0, kb, k1, 1)
    z1 = logits(1, k1)
    x0 = over_z(0, z0)
    k2 = relay(0, kb, k2, 2)
    z2 = logits(2, k2)
    v0 = spread(1, vb, vy, 0)
    p0 = soften(0, x0)
    v1 = spread(1, vb, vy, 1)
    x1 = over_z(1, z1)
    v2 = spread(1, vb, vy, 2)
    p0 = onward(0, p0)
    p1 = soften(1, x1)
    x2 = over_z(2, z2)
    p1 = onward(1, p1)
    v0 = relay(1, vb, v0, 0)
    p2 = soften(2, x2)
    v1 = relay(1, vb, v1, 1)
    p2 = onward(2, p2)
    v2 = relay(1, vb, v2, 2)
    m = mix(0, v0, p0)
    m = m + mix(1, v1, p1)
    m = m + mix(2, v2, p2)
    for p in m:
        p.recv()
    for p in range(RL // 2):
        for hp in range(H // 2):
            a = mxr[2 * hp, :, p * 128:(p + 1) * 128].astype(F32)
            b = mxr[2 * hp + 1, :, p * 128:(p + 1) * 128].astype(F32)
            first, second = pair_lanes(a, b)
            xn[2 * p * CL:(2 * p + 1) * CL, hp * 128:(hp + 1) * 128] = first.astype(BF)
            xn[(2 * p + 1) * CL:(2 * p + 2) * CL, hp * 128:(hp + 1) * 128] = second.astype(BF)
    loads[3].wait()
    for n in range(D // 256):
        wide = dot(xn[...], wro[:, n * 256:(n + 1) * 256])
        for j in (2 * n, 2 * n + 1):
            lanes = slice(j * 128, (j + 1) * 128)
            xf[j] = x[:, lanes].astype(F32) + wide[:, (j - 2 * n) * 128:(j - 2 * n + 1) * 128]

    c_in = []
    for half in range(2):
        for t in range(NS):
            for j in range(D // 128):
                tiles = [xf[j, pl.ds(t * 8 + half * 4 + k, RL, stride=CL), :] for k in range(4)]
                cs[half, t, :, j * 128:(j + 1) * 128] = jnp.concatenate(tiles, axis=0).astype(BF)
        c_in.append([
            Push(log, cs.at[half, sidx[d]], ci.at[half, s], (cs_s, cs_r), (half, d - 1), sdev[d])
            for d in (2, 6, 1, 3, 5, 7, 4)
        ])
        ci[half, s] = cs[half, s]

    row = lax.broadcasted_iota(jnp.int32, (8, 128), 0)
    for t in range(NS):
        tile = jnp.zeros((8, 128), F32)
        for k in range(8):
            tile = jnp.where(row == k, mask[t * 8 + k].astype(F32), tile)
        bias[t * 8:(t + 1) * 8, :] = tile
    live = jnp.concatenate([bias[...], bias[...]], axis=1) > 0.5
    lane = lax.broadcasted_iota(jnp.int32, (1, 256), 1)
    pick = [((lane >= h * 64) & (lane < (h + 1) * 64)).astype(F32) for h in range(4)]

    def attend(tiles):
        scores = []
        for rows, lanes in tiles:
            q = qc[rows, lanes]
            wide = jnp.concatenate([q * pick[h].astype(BF) for h in range(4)], axis=0)
            scores.append(dot(kc[rows, lanes], wide, ((1,), (1,))))
        weights = []
        for st in scores:
            st = jnp.where(live, st * 0.125, -1e30)
            e = jnp.exp(st - jnp.max(st, axis=0, keepdims=True))
            weights.append((e / jnp.sum(e, axis=0, keepdims=True)).astype(BF))
        for (rows, lanes), p in zip(tiles, weights):
            res = dot(p, vc[rows, lanes], ((0,), (0,)))
            mixed = res[0:64] * pick[0]
            for h in range(1, 4):
                mixed = mixed + res[h * 64:(h + 1) * 64] * pick[h]
            cin[rows, lanes] = mixed.astype(BF)

    back = []
    for half in range(2):
        for p in c_in[half]:
            p.recv()
        for k in range(4):
            xo[k * 64:(k + 1) * 64, :] = jnp.concatenate(
                [ci[half, t].astype(F32)[k * 8:(k + 1) * 8] for t in range(NS)], axis=0
            )
        cin[...] = norm(xo[...], gain(gc)).astype(BF)
        for load, weight, into in ((loads[4], wcq, qc), (loads[5], wck, kc), (loads[6], wcv, vc)):
            load.wait()
            into[...] = dot(cin[...], weight[...]).astype(BF)

        @pl.loop(0, 2)
        def _(step):
            attend([
                (chunk(step * 2 + c, 64), slice(g * 256, (g + 1) * 256)) for c in range(2) for g in range(3)
            ])

        loads[7].wait()
        after = (xo[...] + dot(cin[...], wco[...])).astype(BF).astype(F32)
        facc[...] = after
        cin[...] = norm(after, gain(gf)).astype(BF)
        loads[8].wait()
        loads[9].wait()

        @pl.loop(0, FF // D)
        def _(n):
            part_n = chunk(n, D)
            h = dot(cin[...], up[:, part_n])
            hb[...] = (0.5 * h * (1.0 + lax.erf(h * 0.7071067811865476))).astype(BF)
            facc[...] += dot(hb[...], dn[part_n, :])

        for t in range(NS):
            tiles = [facc[k * 64 + t * 8:k * 64 + (t + 1) * 8, :] for k in range(4)]
            co[half, t] = jnp.concatenate(tiles, axis=0).astype(BF)
        back.append([
            Push(log, co.at[half, sidx[d]], cr.at[half, s], (os_, or_), (half, d - 1), sdev[d])
            for d in (2, 6, 1, 3, 5, 7, 4)
        ])
        cr[half, s] = co[half, s]
    for half in range(2):
        for p in back[half]:
            p.recv()
        for t in range(NS):
            for j in range(D // 128):
                wide = cr[half, t, :, j * 128:(j + 1) * 128].astype(F32)
                for k in range(4):
                    xf[j, pl.ds(t * 8 + half * 4 + k, RL, stride=CL), :] = wide[k * 8:(k + 1) * 8]
    for j in range(D // 128):
        out[:, j * 128:(j + 1) * 128] = xf[j].astype(BF)
    finish(log, loads)


def vmem():
    return pl.BlockSpec(memory_space=pltpu.VMEM)


def hbm():
    return pl.BlockSpec(memory_space=pl.ANY)


def pairs_of(*shape):
    return [pltpu.SemaphoreType.DMA(shape)] * 2


def local(
    stream, row_mask, gain_row, row_query, row_key, row_value, row_output,
    gain_column, column_query, column_key, column_value, column_output,
    gain_feed, up_weight, down_weight,
):
    def bf(*shape):
        return pltpu.VMEM(shape, BF)

    def f32(*shape):
        return pltpu.VMEM(shape, F32)

    out = pl.pallas_call(
        layer_kernel,
        out_shape=jax.ShapeDtypeStruct((T, D), BF),
        in_specs=[pl.BlockSpec(memory_space=pltpu.SMEM)] + [vmem()] * 4 + [hbm()] * 10,
        out_specs=vmem(),
        scratch_shapes=[bf(D, D)] * 8 + [
            bf(D, FF), bf(FF, D),
            bf(T, D), f32(T, D), bf(3, H, CL, 512),
            bf(HG, 256, 512), bf(HG, 1024, 512), bf(HG, 1024, 512),
            f32(HG, 256, 1024), bf(HG, 256, 1024), bf(HG, NZ - 1, 64, 1024),
            f32(HG, 32, 1024), f32(HG, 32, 1024), f32(HG, 32, 1024),
            bf(HG, 256, 1024), bf(HG, 256, 512), bf(H, CL, 512),
            bf(2, NS, 32, D), bf(2, NS, 32, D),
            f32(D // 128, T, 128), f32(256, D), bf(256, D), bf(256, D), bf(256, D), bf(256, D), bf(256, D),
            f32(256, D), bf(2, NS, 32, D), bf(2, NS, 32, D), f32(64, 128),
            pltpu.SemaphoreType.DMA((10,)),
        ] + pairs_of(3, HG, NY - 1) + pairs_of(2, HG, 3) + pairs_of(HG, NZ - 1) + pairs_of(HG)
        + pairs_of(HG, 7) + pairs_of(HG, NY - 1) + pairs_of(2, NS - 1) + pairs_of(2, NS - 1),
        compiler_params=pltpu.CompilerParams(
            collective_id=0, has_side_effects=True, vmem_limit_bytes=VMEM_LIMIT
        ),
        name="layer",
    )(
        row_mask, stream.reshape(T, D), gain_row, gain_column, gain_feed,
        row_query, row_key, row_value, row_output,
        column_query, column_key, column_value, column_output, up_weight, down_weight,
    )
    return out.reshape(RL, CL, D)


def solution(mesh):
    return jax.shard_map(
        local,
        mesh=mesh,
        in_specs=(P("seq", "col", None),) + (P(),) * 14,
        out_specs=P("seq", "col", None),
        check_vma=False,
    )
```

```python
import jax
import jax.numpy as jnp
from jax import lax
from jax.experimental import pallas as pl
from jax.experimental.pallas import tpu as pltpu
from jax.sharding import PartitionSpec as P

D = 768
H = 12
DH = 64
FF = 3072
RL = 8
CL = 64
T = RL * CL
NS = 8
NZ = 4
NY = 4
NW = 4
HG = H // NY
BF = jnp.bfloat16
F32 = jnp.float32
MESH = pl.DeviceIdType.MESH
VMEM_LIMIT = 60 * 1024 * 1024


def norm(wide, gain):
    center = wide - jnp.mean(wide, axis=-1, keepdims=True)
    spread = jnp.mean(center * center, axis=-1, keepdims=True)
    return center * lax.rsqrt(spread + 1e-05) * gain


def dot(a, b, dims=((1,), (0,))):
    return lax.dot_general(a, b, (dims, ((), ())), preferred_element_type=F32)


def chunk(index, size):
    return pl.ds(pl.multiple_of(index * size, size), size)


class Load:
    def __init__(self, src, dst, sem):
        self.copy = pltpu.make_async_copy(src, dst, sem)
        self.copy.start()
        self.done = False

    def wait(self):
        if not self.done:
            self.copy.wait()
        self.done = True


class Push:
    def __init__(self, log, src, dst, sems, index, to):
        send, recv = sems
        self.copy = pltpu.make_async_remote_copy(
            src_ref=src, dst_ref=dst, send_sem=send.at[index], recv_sem=recv.at[index],
            device_id=to, device_id_type=MESH,
        )
        self.copy.start()
        self.got = self.left = False
        log.append(self)

    def recv(self):
        if not self.got:
            self.copy.wait_recv()
        self.got = True

    def sent(self):
        if not self.left:
            self.copy.wait_send()
        self.left = True


def finish(log, loads):
    for load in loads:
        load.wait()
    for push in log:
        push.recv()
    for push in log:
        push.sent()


def pair_lanes(a, b):
    low = lax.broadcasted_iota(jnp.int32, a.shape, 1) < DH
    return jnp.where(low, a, pltpu.roll(b, DH, 1)), jnp.where(low, pltpu.roll(a, DH, 1), b)


def layer_kernel(
    mask, x, gr, gc, gf, rq_h, rk_h, rv_h, ro_h, cq_h, ck_h, cv_h, co_h, up_h, dn_h, out,
    wrk, wrq, wrv, wro, wcq, wck, wcv, wco, up, dn,
    xn, acc, pk, qb, kb, vb, part, pb, rs, th, xs, xr, pw, mxs, mxr, cs, ci,
    xf, xo, cin, qc, kc, vc, hb, facc, co, cr, bias,
    lsem, ys, yr, fs, fr, zs, zr, hs, hr, as_, ar, ms, mr, cs_s, cs_r, os_, or_,
):
    s = lax.axis_index("seq")
    col = lax.axis_index("col")
    y, w = lax.div(col, NW), lax.rem(col, NW)
    xl, z = lax.div(s, NZ), lax.rem(s, NZ)
    yidx = [lax.rem(y + d, NY) for d in range(NY)]
    ydev = [(s, yidx[d] * NW + w) for d in range(NY)]
    zidx = [lax.rem(z + d, NZ) for d in range(NZ)]
    zdev = [(xl * NZ + zidx[d], col) for d in range(NZ)]
    xdev = ((1 - xl) * NZ + z, col)
    sidx = [lax.rem(s + d, NS) for d in range(NS)]
    sdev = [(sidx[d], col) for d in range(NS)]
    w_far = lax.rem(w + 2, NW)
    far = (s, y * NW + w_far)
    core = (s, y * NW + w + 1 - 2 * lax.rem(w, 2))

    pairs = (
        (rk_h, wrk), (rq_h, wrq), (rv_h, wrv), (ro_h, wro), (cq_h, wcq), (ck_h, wck), (cv_h, wcv),
        (co_h, wco), (up_h, up), (dn_h, dn),
    )
    loads = [Load(h, v, lsem.at[i]) for i, (h, v) in enumerate(pairs)]
    barrier = pltpu.get_barrier_semaphore()
    peers = ydev[1:] + [far, core] + sdev[1:]
    for peer in peers:
        pl.semaphore_signal(barrier, inc=1, device_id=peer, device_id_type=MESH)
    log = []

    def gain(ref):
        return ref[...].astype(F32).reshape(1, D)

    xn[...] = norm(x[...].astype(F32), gain(gr)).astype(BF)

    def project(kind, weight, load, masked=False):
        load.wait()
        acc[...] = dot(xn[...], weight[...])
        for p in range(RL // 2):
            for hp in range(H // 2):
                a = acc[2 * p * CL:(2 * p + 1) * CL, hp * 128:(hp + 1) * 128]
                b = acc[(2 * p + 1) * CL:(2 * p + 2) * CL, hp * 128:(hp + 1) * 128]
                if masked:
                    a = a * mask[s * RL + 2 * p].astype(F32)
                    b = b * mask[s * RL + 2 * p + 1].astype(F32)
                first, second = pair_lanes(a, b)
                pk[kind, 2 * hp, :, p * 128:(p + 1) * 128] = first.astype(BF)
                pk[kind, 2 * hp + 1, :, p * 128:(p + 1) * 128] = second.astype(BF)

    def over_y(kind, into, base, g):
        rows = chunk(base, CL)
        pushes = [
            Push(log, pk.at[kind, yidx[d] * HG + g], into.at[g, rows], (ys, yr), (kind, g, d - 1), ydev[d])
            for d in (2, 1, 3)
        ]
        into[g, rows, :] = pk[kind, y * HG + g]
        return pushes

    def spread(kind, ref, pushes, g):
        for p in pushes[g]:
            p.recv()
        block = ref.at[g, chunk(w, 256)]
        return (
            Push(log, block, block, (fs, fr), (kind, g, 0), far),
            Push(log, block, block, (fs, fr), (kind, g, 1), core),
        )

    def relay(kind, ref, pushes, g):
        pushes[0].recv()
        block = ref.at[g, chunk(w_far, 256)]
        last = Push(log, block, block, (fs, fr), (kind, g, 2), core)
        pushes[1].recv()
        return last

    def logits(g, last):
        for p in qy[g]:
            p.recv()
        last.recv()
        for j in range(4):
            block = dot(qb[g], kb[g, j * 256:(j + 1) * 256, :], ((1,), (1,)))
            part[g, :, j * 256:(j + 1) * 256] = block * (1.0 / 64.0)
        raw = part[g]
        e = jnp.exp(raw - jnp.max(raw, axis=-1, keepdims=True))
        center = jnp.sum(e * raw, axis=-1, keepdims=True) / jnp.sum(e, axis=-1, keepdims=True)
        shifted = raw - center
        part[g] = shifted
        pb[g] = shifted.astype(BF)
        return [
            Push(log, pb.at[g, chunk(zidx[d], 64)], rs.at[g, d - 1], (zs, zr), (g, d - 1), zdev[d]) for d in (2, 1, 3)
        ]

    def over_z(g, pushes):
        for p in pushes:
            p.recv()
        total = part[g, chunk(z, 64), :]
        for d in range(NZ - 1):
            total = total + rs[g, d].astype(F32)
        th[g] = total
        xs[g] = total.astype(BF)
        return Push(log, xs.at[g], xr.at[g], (hs, hr), (g,), xdev)

    def soften(g, push):
        push.recv()
        total = th[g] + xr[g].astype(F32)
        e = jnp.exp(total - jnp.max(total, axis=-1, keepdims=True))
        rows = chunk(z, 64)
        pw[g, rows, :] = (e / jnp.sum(e, axis=-1, keepdims=True)).astype(BF)
        block = pw.at[g, rows]
        return [Push(log, block, block, (as_, ar), (g, d - 1), zdev[d]) for d in (2, 1, 3)]

    def mix(g, last, pushes):
        last.recv()
        for p in pushes:
            p.recv()
        mxs[g] = dot(pw[g], vb[g]).astype(BF)
        got = [
            Push(log, mxs.at[g, chunk(yidx[d], CL)], mxr.at[y * HG + g], (ms, mr), (g, d - 1), ydev[d])
            for d in (2, 1, 3)
        ]
        mxr[y * HG + g] = mxs[g, chunk(y, CL), :]
        return got

    own = w * NY + y
    ky, qy, vy = [None] * HG, [None] * HG, [None] * HG
    project(0, wrk, loads[0])
    pl.semaphore_wait(barrier, len(peers))
    ky[0] = over_y(0, kb, own, 0)
    project(1, wrq, loads[1], masked=True)
    qy[0] = over_y(1, qb, y, 0)
    for g in range(1, HG):
        ky[g] = over_y(0, kb, own, g)
        qy[g] = over_y(1, qb, y, g)
    k0 = spread(0, kb, ky, 0)
    project(2, wrv, loads[2])
    for g in range(HG):
        vy[g] = over_y(2, vb, own, g)
    k1 = spread(0, kb, ky, 1)
    k0 = relay(0, kb, k0, 0)
    z0 = logits(0, k0)
    k2 = spread(0, kb, ky, 2)
    k1 = relay(0, kb, k1, 1)
    z1 = logits(1, k1)
    x0 = over_z(0, z0)
    k2 = relay(0, kb, k2, 2)
    z2 = logits(2, k2)
    x1 = over_z(1, z1)
    v0 = spread(1, vb, vy, 0)
    p0 = soften(0, x0)
    p1 = soften(1, x1)
    x2 = over_z(2, z2)
    v1 = spread(1, vb, vy, 1)
    v2 = spread(1, vb, vy, 2)
    p2 = soften(2, x2)
    v0 = relay(1, vb, v0, 0)
    m = mix(0, v0, p0)
    v1 = relay(1, vb, v1, 1)
    m = m + mix(1, v1, p1)
    v2 = relay(1, vb, v2, 2)
    m = m + mix(2, v2, p2)
    for p in m:
        p.recv()
    for p in range(RL // 2):
        for hp in range(H // 2):
            a = mxr[2 * hp, :, p * 128:(p + 1) * 128].astype(F32)
            b = mxr[2 * hp + 1, :, p * 128:(p + 1) * 128].astype(F32)
            first, second = pair_lanes(a, b)
            xn[2 * p * CL:(2 * p + 1) * CL, hp * 128:(hp + 1) * 128] = first.astype(BF)
            xn[(2 * p + 1) * CL:(2 * p + 2) * CL, hp * 128:(hp + 1) * 128] = second.astype(BF)
    loads[3].wait()
    for n in range(D // 256):
        wide = dot(xn[...], wro[:, n * 256:(n + 1) * 256])
        for j in (2 * n, 2 * n + 1):
            lanes = slice(j * 128, (j + 1) * 128)
            xf[j] = x[:, lanes].astype(F32) + wide[:, (j - 2 * n) * 128:(j - 2 * n + 1) * 128]

    c_in = []
    for half in range(2):
        for t in range(NS):
            for j in range(D // 128):
                tiles = [xf[j, pl.ds(t * 8 + half * 4 + k, RL, stride=CL), :] for k in range(4)]
                cs[half, t, :, j * 128:(j + 1) * 128] = jnp.concatenate(tiles, axis=0).astype(BF)
        c_in.append([
            Push(log, cs.at[half, sidx[d]], ci.at[half, s], (cs_s, cs_r), (half, d - 1), sdev[d])
            for d in (2, 6, 1, 3, 5, 7, 4)
        ])
        ci[half, s] = cs[half, s]

    row = lax.broadcasted_iota(jnp.int32, (8, 128), 0)
    for t in range(NS):
        tile = jnp.zeros((8, 128), F32)
        for k in range(8):
            tile = jnp.where(row == k, mask[t * 8 + k].astype(F32), tile)
        bias[t * 8:(t + 1) * 8, :] = tile
    live = jnp.concatenate([bias[...], bias[...]], axis=1) > 0.5
    lane = lax.broadcasted_iota(jnp.int32, (1, 256), 1)
    pick = [((lane >= h * 64) & (lane < (h + 1) * 64)).astype(F32) for h in range(4)]

    def attend(tiles):
        scores = []
        for rows, lanes in tiles:
            q = qc[rows, lanes]
            wide = jnp.concatenate([q * pick[h].astype(BF) for h in range(4)], axis=0)
            scores.append(dot(kc[rows, lanes], wide, ((1,), (1,))))
        weights = []
        for st in scores:
            st = jnp.where(live, st * 0.125, -1e30)
            e = jnp.exp(st - jnp.max(st, axis=0, keepdims=True))
            weights.append((e / jnp.sum(e, axis=0, keepdims=True)).astype(BF))
        for (rows, lanes), p in zip(tiles, weights):
            res = dot(p, vc[rows, lanes], ((0,), (0,)))
            mixed = res[0:64] * pick[0]
            for h in range(1, 4):
                mixed = mixed + res[h * 64:(h + 1) * 64] * pick[h]
            cin[rows, lanes] = mixed.astype(BF)

    back = []
    for half in range(2):
        for p in c_in[half]:
            p.recv()
        for k in range(4):
            xo[k * 64:(k + 1) * 64, :] = jnp.concatenate(
                [ci[half, t].astype(F32)[k * 8:(k + 1) * 8] for t in range(NS)], axis=0
            )
        cin[...] = norm(xo[...], gain(gc)).astype(BF)
        for load, weight, into in ((loads[4], wcq, qc), (loads[5], wck, kc), (loads[6], wcv, vc)):
            load.wait()
            into[...] = dot(cin[...], weight[...]).astype(BF)

        @pl.loop(0, 2)
        def _(step):
            attend([
                (chunk(step * 2 + c, 64), slice(g * 256, (g + 1) * 256)) for c in range(2) for g in range(3)
            ])

        loads[7].wait()
        after = (xo[...] + dot(cin[...], wco[...])).astype(BF).astype(F32)
        facc[...] = after
        cin[...] = norm(after, gain(gf)).astype(BF)
        loads[8].wait()
        loads[9].wait()

        @pl.loop(0, FF // D)
        def _(n):
            part_n = chunk(n, D)
            h = dot(cin[...], up[:, part_n])
            hb[...] = (0.5 * h * (1.0 + lax.erf(h * 0.7071067811865476))).astype(BF)
            facc[...] += dot(hb[...], dn[part_n, :])

        for t in range(NS):
            tiles = [facc[k * 64 + t * 8:k * 64 + (t + 1) * 8, :] for k in range(4)]
            co[half, t] = jnp.concatenate(tiles, axis=0).astype(BF)
        back.append([
            Push(log, co.at[half, sidx[d]], cr.at[half, s], (os_, or_), (half, d - 1), sdev[d])
            for d in (2, 6, 1, 3, 5, 7, 4)
        ])
        cr[half, s] = co[half, s]
    for half in range(2):
        for p in back[half]:
            p.recv()
        for t in range(NS):
            for j in range(D // 128):
                wide = cr[half, t, :, j * 128:(j + 1) * 128].astype(F32)
                for k in range(4):
                    xf[j, pl.ds(t * 8 + half * 4 + k, RL, stride=CL), :] = wide[k * 8:(k + 1) * 8]
    for j in range(D // 128):
        out[:, j * 128:(j + 1) * 128] = xf[j].astype(BF)
    finish(log, loads)


def vmem():
    return pl.BlockSpec(memory_space=pltpu.VMEM)


def hbm():
    return pl.BlockSpec(memory_space=pl.ANY)


def pairs_of(*shape):
    return [pltpu.SemaphoreType.DMA(shape)] * 2


def local(
    stream, row_mask, gain_row, row_query, row_key, row_value, row_output,
    gain_column, column_query, column_key, column_value, column_output,
    gain_feed, up_weight, down_weight,
):
    def bf(*shape):
        return pltpu.VMEM(shape, BF)

    def f32(*shape):
        return pltpu.VMEM(shape, F32)

    out = pl.pallas_call(
        layer_kernel,
        out_shape=jax.ShapeDtypeStruct((T, D), BF),
        in_specs=[pl.BlockSpec(memory_space=pltpu.SMEM)] + [vmem()] * 4 + [hbm()] * 10,
        out_specs=vmem(),
        scratch_shapes=[bf(D, D)] * 8 + [
            bf(D, FF), bf(FF, D),
            bf(T, D), f32(T, D), bf(3, H, CL, 512),
            bf(HG, 256, 512), bf(HG, 1024, 512), bf(HG, 1024, 512),
            f32(HG, 256, 1024), bf(HG, 256, 1024), bf(HG, NZ - 1, 64, 1024),
            f32(HG, 64, 1024), bf(HG, 64, 1024), bf(HG, 64, 1024),
            bf(HG, 256, 1024), bf(HG, 256, 512), bf(H, CL, 512),
            bf(2, NS, 32, D), bf(2, NS, 32, D),
            f32(D // 128, T, 128), f32(256, D), bf(256, D), bf(256, D), bf(256, D), bf(256, D), bf(256, D),
            f32(256, D), bf(2, NS, 32, D), bf(2, NS, 32, D), f32(64, 128),
            pltpu.SemaphoreType.DMA((10,)),
        ] + pairs_of(3, HG, NY - 1) + pairs_of(2, HG, 3) + pairs_of(HG, NZ - 1) + pairs_of(HG)
        + pairs_of(HG, NZ - 1) + pairs_of(HG, NY - 1) + pairs_of(2, NS - 1) + pairs_of(2, NS - 1),
        compiler_params=pltpu.CompilerParams(
            collective_id=0, has_side_effects=True, vmem_limit_bytes=VMEM_LIMIT
        ),
        name="layer",
    )(
        row_mask, stream.reshape(T, D), gain_row, gain_column, gain_feed,
        row_query, row_key, row_value, row_output,
        column_query, column_key, column_value, column_output, up_weight, down_weight,
    )
    return out.reshape(RL, CL, D)


def solution(mesh):
    return jax.shard_map(
        local,
        mesh=mesh,
        in_specs=(P("seq", "col", None),) + (P(),) * 14,
        out_specs=P("seq", "col", None),
        check_vma=False,
    )
```

```python
import jax
import jax.numpy as jnp
from jax import lax
from jax.experimental import pallas as pl
from jax.experimental.pallas import tpu as pltpu
from jax.sharding import PartitionSpec as P

D = 768
H = 12
DH = 64
FF = 3072
RL = 8
CL = 64
T = RL * CL
NS = 8
NZ = 4
NY = 4
NW = 4
HG = H // NY
BF = jnp.bfloat16
F32 = jnp.float32
MESH = pl.DeviceIdType.MESH
VMEM_LIMIT = 60 * 1024 * 1024


def norm(wide, gain):
    center = wide - jnp.mean(wide, axis=-1, keepdims=True)
    spread = jnp.mean(center * center, axis=-1, keepdims=True)
    return center * lax.rsqrt(spread + 1e-05) * gain


def dot(a, b, dims=((1,), (0,))):
    return lax.dot_general(a, b, (dims, ((), ())), preferred_element_type=F32)


def chunk(index, size):
    return pl.ds(pl.multiple_of(index * size, size), size)


class Load:
    def __init__(self, src, dst, sem):
        self.copy = pltpu.make_async_copy(src, dst, sem)
        self.copy.start()
        self.done = False

    def wait(self):
        if not self.done:
            self.copy.wait()
        self.done = True


class Push:
    def __init__(self, log, src, dst, sems, index, to):
        send, recv = sems
        self.copy = pltpu.make_async_remote_copy(
            src_ref=src, dst_ref=dst, send_sem=send.at[index], recv_sem=recv.at[index],
            device_id=to, device_id_type=MESH,
        )
        self.copy.start()
        self.got = self.left = False
        log.append(self)

    def recv(self):
        if not self.got:
            self.copy.wait_recv()
        self.got = True

    def sent(self):
        if not self.left:
            self.copy.wait_send()
        self.left = True


def finish(log, loads):
    for load in loads:
        load.wait()
    for push in log:
        push.recv()
    for push in log:
        push.sent()


def pair_lanes(a, b):
    low = lax.broadcasted_iota(jnp.int32, a.shape, 1) < DH
    return jnp.where(low, a, pltpu.roll(b, DH, 1)), jnp.where(low, pltpu.roll(a, DH, 1), b)


def layer_kernel(
    mask, x, gr, gc, gf, rq_h, rk_h, rv_h, ro_h, cq_h, ck_h, cv_h, co_h, up_h, dn_h, out,
    wrk, wrq, wrv, wro, wcq, wck, wcv, wco, up, dn,
    xn, acc, pk, qb, kb, vb, part, pb, rs, th, xs, xr, pw, mxs, mxr, cs, ci,
    xf, xo, cin, qc, kc, vc, hb, facc, co, cr, bias,
    lsem, ys, yr, fs, fr, ps, pr, zs, zr, hs, hr, as_, ar, ms, mr, cs_s, cs_r, os_, or_,
):
    s = lax.axis_index("seq")
    col = lax.axis_index("col")
    y, w = lax.div(col, NW), lax.rem(col, NW)
    xl, z = lax.div(s, NZ), lax.rem(s, NZ)
    yidx = [lax.rem(y + d, NY) for d in range(NY)]
    ydev = [(s, yidx[d] * NW + w) for d in range(NY)]
    zidx = [lax.rem(z + d, NZ) for d in range(NZ)]
    zdev = [(xl * NZ + zidx[d], col) for d in range(NZ)]
    xdev = ((1 - xl) * NZ + z, col)
    sidx = [lax.rem(s + d, NS) for d in range(NS)]
    sdev = [(sidx[d], col) for d in range(NS)]
    w_far = lax.rem(w + 2, NW)
    far = (s, y * NW + w_far)
    core = (s, y * NW + w + 1 - 2 * lax.rem(w, 2))

    pairs = (
        (rk_h, wrk), (rq_h, wrq), (rv_h, wrv), (ro_h, wro), (cq_h, wcq), (ck_h, wck), (cv_h, wcv),
        (co_h, wco), (up_h, up), (dn_h, dn),
    )
    loads = [Load(h, v, lsem.at[i]) for i, (h, v) in enumerate(pairs)]
    barrier = pltpu.get_barrier_semaphore()
    peers = ydev[1:] + [far, core] + sdev[1:]
    for peer in peers:
        pl.semaphore_signal(barrier, inc=1, device_id=peer, device_id_type=MESH)
    log = []

    def gain(ref):
        return ref[...].astype(F32).reshape(1, D)

    xn[...] = norm(x[...].astype(F32), gain(gr)).astype(BF)

    def project(kind, weight, load, masked=False):
        load.wait()
        acc[...] = dot(xn[...], weight[...])
        for p in range(RL // 2):
            for hp in range(H // 2):
                a = acc[2 * p * CL:(2 * p + 1) * CL, hp * 128:(hp + 1) * 128]
                b = acc[(2 * p + 1) * CL:(2 * p + 2) * CL, hp * 128:(hp + 1) * 128]
                if masked:
                    a = a * mask[s * RL + 2 * p].astype(F32)
                    b = b * mask[s * RL + 2 * p + 1].astype(F32)
                first, second = pair_lanes(a, b)
                pk[kind, 2 * hp, :, p * 128:(p + 1) * 128] = first.astype(BF)
                pk[kind, 2 * hp + 1, :, p * 128:(p + 1) * 128] = second.astype(BF)

    def over_y(kind, into, base, g):
        rows = chunk(base, CL)
        pushes = [
            Push(log, pk.at[kind, yidx[d] * HG + g], into.at[g, rows], (ys, yr), (kind, g, d - 1), ydev[d])
            for d in (2, 1, 3)
        ]
        into[g, rows, :] = pk[kind, y * HG + g]
        return pushes

    def spread(kind, ref, pushes, g):
        for p in pushes[g]:
            p.recv()
        block = ref.at[g, chunk(w, 256)]
        return (
            Push(log, block, block, (fs, fr), (kind, g, 0), far),
            Push(log, block, block, (fs, fr), (kind, g, 1), core),
        )

    def piece(index, i):
        block = kb.at[0, chunk(w * NY + index, CL)]
        return (
            Push(log, block, block, (ps, pr), (0, i), far),
            Push(log, block, block, (ps, pr), (1, i), core),
        )

    def join(pieces):
        for a, b in pieces:
            a.recv()
        block = kb.at[0, chunk(w_far, 256)]
        last = Push(log, block, block, (fs, fr), (0, 0, 2), core)
        for a, b in pieces:
            b.recv()
        return last

    def relay(kind, ref, pushes, g):
        pushes[0].recv()
        block = ref.at[g, chunk(w_far, 256)]
        last = Push(log, block, block, (fs, fr), (kind, g, 2), core)
        pushes[1].recv()
        return last

    def logits(g, last):
        for p in qy[g]:
            p.recv()
        last.recv()
        for j in range(4):
            block = dot(qb[g], kb[g, j * 256:(j + 1) * 256, :], ((1,), (1,)))
            part[g, :, j * 256:(j + 1) * 256] = block * (1.0 / 64.0)
        raw = part[g]
        e = jnp.exp(raw - jnp.max(raw, axis=-1, keepdims=True))
        center = jnp.sum(e * raw, axis=-1, keepdims=True) / jnp.sum(e, axis=-1, keepdims=True)
        shifted = raw - center
        part[g] = shifted
        pb[g] = shifted.astype(BF)
        return [
            Push(log, pb.at[g, chunk(zidx[d], 64)], rs.at[g, d - 1], (zs, zr), (g, d - 1), zdev[d]) for d in (2, 1, 3)
        ]

    def over_z(g, pushes):
        for p in pushes:
            p.recv()
        total = part[g, chunk(z, 64), :]
        for d in range(NZ - 1):
            total = total + rs[g, d].astype(F32)
        th[g] = total
        xs[g] = total.astype(BF)
        return Push(log, xs.at[g], xr.at[g], (hs, hr), (g,), xdev)

    def soften(g, push):
        push.recv()
        total = th[g] + xr[g].astype(F32)
        e = jnp.exp(total - jnp.max(total, axis=-1, keepdims=True))
        rows = chunk(z, 64)
        pw[g, rows, :] = (e / jnp.sum(e, axis=-1, keepdims=True)).astype(BF)
        block = pw.at[g, rows]
        return [
            Push(log, block, block, (as_, ar), (g, 0), zdev[1]),
            Push(log, block, block, (as_, ar), (g, 1), zdev[3]),
        ]

    def onward(g, pushes):
        pushes[0].recv()
        first = pw.at[g, chunk(zidx[3] * 2, 32)]
        a = Push(log, first, first, (as_, ar), (g, 2), zdev[1])
        pushes[1].recv()
        second = pw.at[g, chunk(zidx[1] * 2 + 1, 32)]
        b = Push(log, second, second, (as_, ar), (g, 3), zdev[3])
        return [a, b]

    def mix(g, last, pushes):
        last.recv()
        for p in pushes:
            p.recv()
        mxs[g] = dot(pw[g], vb[g]).astype(BF)
        got = [
            Push(log, mxs.at[g, chunk(yidx[d], CL)], mxr.at[y * HG + g], (ms, mr), (g, d - 1), ydev[d])
            for d in (2, 1, 3)
        ]
        mxr[y * HG + g] = mxs[g, chunk(y, CL), :]
        return got

    own = w * NY + y
    ky, qy, vy = [None] * HG, [None] * HG, [None] * HG
    project(0, wrk, loads[0])
    pl.semaphore_wait(barrier, len(peers))
    ky[0] = over_y(0, kb, own, 0)
    k0 = [piece(y, 0)]
    project(1, wrq, loads[1], masked=True)
    ky[1] = over_y(0, kb, own, 1)
    qy[0] = over_y(1, qb, y, 0)
    ky[2] = over_y(0, kb, own, 2)
    qy[1] = over_y(1, qb, y, 1)
    qy[2] = over_y(1, qb, y, 2)
    for push, d in ((ky[0][1], 3), (ky[0][2], 1), (ky[0][0], 2)):
        push.recv()
        k0.append(piece(yidx[d], d))
    project(2, wrv, loads[2])
    for g in range(HG):
        vy[g] = over_y(2, vb, own, g)
    k1 = spread(0, kb, ky, 1)
    k0 = join(k0)
    z0 = logits(0, k0)
    k2 = spread(0, kb, ky, 2)
    k1 = relay(0, kb, k1, 1)
    z1 = logits(1, k1)
    x0 = over_z(0, z0)
    k2 = relay(0, kb, k2, 2)
    v0 = spread(1, vb, vy, 0)
    z2 = logits(2, k2)
    p0 = soften(0, x0)
    x1 = over_z(1, z1)
    x2 = over_z(2, z2)
    v1 = spread(1, vb, vy, 1)
    v2 = spread(1, vb, vy, 2)
    p1 = soften(1, x1)
    p0 = onward(0, p0)
    v0 = relay(1, vb, v0, 0)
    p2 = soften(2, x2)
    m = mix(0, v0, p0)
    p1 = onward(1, p1)
    p2 = onward(2, p2)
    v1 = relay(1, vb, v1, 1)
    m = m + mix(1, v1, p1)
    v2 = relay(1, vb, v2, 2)
    m = m + mix(2, v2, p2)
    for p in m:
        p.recv()
    for p in range(RL // 2):
        for hp in range(H // 2):
            a = mxr[2 * hp, :, p * 128:(p + 1) * 128].astype(F32)
            b = mxr[2 * hp + 1, :, p * 128:(p + 1) * 128].astype(F32)
            first, second = pair_lanes(a, b)
            xn[2 * p * CL:(2 * p + 1) * CL, hp * 128:(hp + 1) * 128] = first.astype(BF)
            xn[(2 * p + 1) * CL:(2 * p + 2) * CL, hp * 128:(hp + 1) * 128] = second.astype(BF)
    loads[3].wait()
    for n in range(D // 256):
        wide = dot(xn[...], wro[:, n * 256:(n + 1) * 256])
        for j in (2 * n, 2 * n + 1):
            lanes = slice(j * 128, (j + 1) * 128)
            xf[j] = x[:, lanes].astype(F32) + wide[:, (j - 2 * n) * 128:(j - 2 * n + 1) * 128]

    c_in = []
    for half in range(2):
        for t in range(NS):
            for j in range(D // 128):
                tiles = [xf[j, pl.ds(t * 8 + half * 4 + k, RL, stride=CL), :] for k in range(4)]
                cs[half, t, :, j * 128:(j + 1) * 128] = jnp.concatenate(tiles, axis=0).astype(BF)
        c_in.append([
            Push(log, cs.at[half, sidx[d]], ci.at[half, s], (cs_s, cs_r), (half, d - 1), sdev[d])
            for d in (2, 6, 1, 3, 5, 7, 4)
        ])
        ci[half, s] = cs[half, s]

    row = lax.broadcasted_iota(jnp.int32, (8, 128), 0)
    for t in range(NS):
        tile = jnp.zeros((8, 128), F32)
        for k in range(8):
            tile = jnp.where(row == k, mask[t * 8 + k].astype(F32), tile)
        bias[t * 8:(t + 1) * 8, :] = tile
    live = jnp.concatenate([bias[...], bias[...]], axis=1) > 0.5
    lane = lax.broadcasted_iota(jnp.int32, (1, 256), 1)
    pick = [((lane >= h * 64) & (lane < (h + 1) * 64)).astype(F32) for h in range(4)]

    def attend(tiles):
        scores = []
        for rows, lanes in tiles:
            q = qc[rows, lanes]
            wide = jnp.concatenate([q * pick[h].astype(BF) for h in range(4)], axis=0)
            scores.append(dot(kc[rows, lanes], wide, ((1,), (1,))))
        weights = []
        for st in scores:
            st = jnp.where(live, st * 0.125, -1e30)
            e = jnp.exp(st - jnp.max(st, axis=0, keepdims=True))
            weights.append((e / jnp.sum(e, axis=0, keepdims=True)).astype(BF))
        for (rows, lanes), p in zip(tiles, weights):
            res = dot(p, vc[rows, lanes], ((0,), (0,)))
            mixed = res[0:64] * pick[0]
            for h in range(1, 4):
                mixed = mixed + res[h * 64:(h + 1) * 64] * pick[h]
            cin[rows, lanes] = mixed.astype(BF)

    back = []
    for half in range(2):
        for p in c_in[half]:
            p.recv()
        for k in range(4):
            xo[k * 64:(k + 1) * 64, :] = jnp.concatenate(
                [ci[half, t].astype(F32)[k * 8:(k + 1) * 8] for t in range(NS)], axis=0
            )
        cin[...] = norm(xo[...], gain(gc)).astype(BF)
        for load, weight, into in ((loads[4], wcq, qc), (loads[5], wck, kc), (loads[6], wcv, vc)):
            load.wait()
            into[...] = dot(cin[...], weight[...]).astype(BF)

        @pl.loop(0, 2)
        def _(step):
            attend([
                (chunk(step * 2 + c, 64), slice(g * 256, (g + 1) * 256)) for c in range(2) for g in range(3)
            ])

        loads[7].wait()
        after = (xo[...] + dot(cin[...], wco[...])).astype(BF).astype(F32)
        facc[...] = after
        cin[...] = norm(after, gain(gf)).astype(BF)
        loads[8].wait()
        loads[9].wait()

        @pl.loop(0, FF // D)
        def _(n):
            part_n = chunk(n, D)
            h = dot(cin[...], up[:, part_n])
            hb[...] = (0.5 * h * (1.0 + lax.erf(h * 0.7071067811865476))).astype(BF)
            facc[...] += dot(hb[...], dn[part_n, :])

        for t in range(NS):
            tiles = [facc[k * 64 + t * 8:k * 64 + (t + 1) * 8, :] for k in range(4)]
            co[half, t] = jnp.concatenate(tiles, axis=0).astype(BF)
        back.append([
            Push(log, co.at[half, sidx[d]], cr.at[half, s], (os_, or_), (half, d - 1), sdev[d])
            for d in (2, 6, 1, 3, 5, 7, 4)
        ])
        cr[half, s] = co[half, s]
    for half in range(2):
        for p in back[half]:
            p.recv()
        for t in range(NS):
            for j in range(D // 128):
                wide = cr[half, t, :, j * 128:(j + 1) * 128].astype(F32)
                for k in range(4):
                    xf[j, pl.ds(t * 8 + half * 4 + k, RL, stride=CL), :] = wide[k * 8:(k + 1) * 8]
    for j in range(D // 128):
        out[:, j * 128:(j + 1) * 128] = xf[j].astype(BF)
    finish(log, loads)


def vmem():
    return pl.BlockSpec(memory_space=pltpu.VMEM)


def hbm():
    return pl.BlockSpec(memory_space=pl.ANY)


def pairs_of(*shape):
    return [pltpu.SemaphoreType.DMA(shape)] * 2


def local(
    stream, row_mask, gain_row, row_query, row_key, row_value, row_output,
    gain_column, column_query, column_key, column_value, column_output,
    gain_feed, up_weight, down_weight,
):
    def bf(*shape):
        return pltpu.VMEM(shape, BF)

    def f32(*shape):
        return pltpu.VMEM(shape, F32)

    out = pl.pallas_call(
        layer_kernel,
        out_shape=jax.ShapeDtypeStruct((T, D), BF),
        in_specs=[pl.BlockSpec(memory_space=pltpu.SMEM)] + [vmem()] * 4 + [hbm()] * 10,
        out_specs=vmem(),
        scratch_shapes=[bf(D, D)] * 8 + [
            bf(D, FF), bf(FF, D),
            bf(T, D), f32(T, D), bf(3, H, CL, 512),
            bf(HG, 256, 512), bf(HG, 1024, 512), bf(HG, 1024, 512),
            f32(HG, 256, 1024), bf(HG, 256, 1024), bf(HG, NZ - 1, 64, 1024),
            f32(HG, 64, 1024), bf(HG, 64, 1024), bf(HG, 64, 1024),
            bf(HG, 256, 1024), bf(HG, 256, 512), bf(H, CL, 512),
            bf(2, NS, 32, D), bf(2, NS, 32, D),
            f32(D // 128, T, 128), f32(256, D), bf(256, D), bf(256, D), bf(256, D), bf(256, D), bf(256, D),
            f32(256, D), bf(2, NS, 32, D), bf(2, NS, 32, D), f32(64, 128),
            pltpu.SemaphoreType.DMA((10,)),
        ] + pairs_of(3, HG, NY - 1) + pairs_of(2, HG, 3) + pairs_of(2, NY) + pairs_of(HG, NZ - 1)
        + pairs_of(HG) + pairs_of(HG, 4) + pairs_of(HG, NY - 1) + pairs_of(2, NS - 1) + pairs_of(2, NS - 1),
        compiler_params=pltpu.CompilerParams(
            collective_id=0, has_side_effects=True, vmem_limit_bytes=VMEM_LIMIT
        ),
        name="layer",
    )(
        row_mask, stream.reshape(T, D), gain_row, gain_column, gain_feed,
        row_query, row_key, row_value, row_output,
        column_query, column_key, column_value, column_output, up_weight, down_weight,
    )
    return out.reshape(RL, CL, D)


def solution(mesh):
    return jax.shard_map(
        local,
        mesh=mesh,
        in_specs=(P("seq", "col", None),) + (P(),) * 14,
        out_specs=P("seq", "col", None),
        check_vma=False,
    )
```

```python
import jax
import jax.numpy as jnp
from jax import lax
from jax.experimental import pallas as pl
from jax.experimental.pallas import tpu as pltpu
from jax.sharding import PartitionSpec as P

D = 768
H = 12
DH = 64
FF = 3072
RL = 8
CL = 64
T = RL * CL
NS = 8
NZ = 4
NY = 4
NW = 4
HG = H // NY
BF = jnp.bfloat16
F32 = jnp.float32
MESH = pl.DeviceIdType.MESH
VMEM_LIMIT = 60 * 1024 * 1024


def norm(wide, gain):
    center = wide - jnp.mean(wide, axis=-1, keepdims=True)
    spread = jnp.mean(center * center, axis=-1, keepdims=True)
    return center * lax.rsqrt(spread + 1e-05) * gain


def dot(a, b, dims=((1,), (0,))):
    return lax.dot_general(a, b, (dims, ((), ())), preferred_element_type=F32)


def chunk(index, size):
    return pl.ds(pl.multiple_of(index * size, size), size)


class Load:
    def __init__(self, src, dst, sem):
        self.copy = pltpu.make_async_copy(src, dst, sem)
        self.copy.start()
        self.done = False

    def wait(self):
        if not self.done:
            self.copy.wait()
        self.done = True


class Push:
    def __init__(self, log, src, dst, sems, index, to):
        send, recv = sems
        self.copy = pltpu.make_async_remote_copy(
            src_ref=src, dst_ref=dst, send_sem=send.at[index], recv_sem=recv.at[index],
            device_id=to, device_id_type=MESH,
        )
        self.copy.start()
        self.got = self.left = False
        log.append(self)

    def recv(self):
        if not self.got:
            self.copy.wait_recv()
        self.got = True

    def sent(self):
        if not self.left:
            self.copy.wait_send()
        self.left = True


def finish(log, loads):
    for load in loads:
        load.wait()
    for push in log:
        push.recv()
    for push in log:
        push.sent()


def pair_lanes(a, b):
    low = lax.broadcasted_iota(jnp.int32, a.shape, 1) < DH
    return jnp.where(low, a, pltpu.roll(b, DH, 1)), jnp.where(low, pltpu.roll(a, DH, 1), b)


def layer_kernel(
    mask_h, x, gr, gc, gf, rq_h, rk_h, rv_h, ro_h, cq_h, ck_h, cv_h, co_h, up_h, dn_h, out,
    mask, wrk, wrq, wrv, wro, wcq, wck, wcv, wco, up, dn,
    xn, acc, pk, qb, kb, vb, part, pb, rs, th, xs, xr, pw, mxs, mxr, cs, ci,
    xf, xo, cin, qc, kc, vc, hb, facc, co, cr, bias,
    lsem, ys, yr, fs, fr, ps, pr, zs, zr, hs, hr, as_, ar, ms, mr, cs_s, cs_r, os_, or_,
):
    s = lax.axis_index("seq")
    col = lax.axis_index("col")
    y, w = lax.div(col, NW), lax.rem(col, NW)
    xl, z = lax.div(s, NZ), lax.rem(s, NZ)
    yidx = [lax.rem(y + d, NY) for d in range(NY)]
    ydev = [(s, yidx[d] * NW + w) for d in range(NY)]
    zidx = [lax.rem(z + d, NZ) for d in range(NZ)]
    zdev = [(xl * NZ + zidx[d], col) for d in range(NZ)]
    xdev = ((1 - xl) * NZ + z, col)
    sidx = [lax.rem(s + d, NS) for d in range(NS)]
    sdev = [(sidx[d], col) for d in range(NS)]
    w_far = lax.rem(w + 2, NW)
    far = (s, y * NW + w_far)
    core = (s, y * NW + w + 1 - 2 * lax.rem(w, 2))

    pairs = (
        (rk_h, wrk), (rq_h, wrq), (rv_h, wrv), (ro_h, wro), (cq_h, wcq), (ck_h, wck), (cv_h, wcv),
        (co_h, wco), (up_h, up), (dn_h, dn),
    )
    loads = [Load(h, v, lsem.at[i]) for i, (h, v) in enumerate(pairs)]
    mask_load = Load(mask_h, mask, lsem.at[10])
    loads.append(mask_load)
    barrier = pltpu.get_barrier_semaphore()
    peers = ydev[1:] + [far, core] + sdev[1:]
    for peer in peers:
        pl.semaphore_signal(barrier, inc=1, device_id=peer, device_id_type=MESH)
    log = []

    def gain(ref):
        return ref[...].astype(F32).reshape(1, D)

    xn[...] = norm(x[...].astype(F32), gain(gr)).astype(BF)

    def project(kind, weight, load, masked=False):
        load.wait()
        acc[...] = dot(xn[...], weight[...])
        for p in range(RL // 2):
            for hp in range(H // 2):
                a = acc[2 * p * CL:(2 * p + 1) * CL, hp * 128:(hp + 1) * 128]
                b = acc[(2 * p + 1) * CL:(2 * p + 2) * CL, hp * 128:(hp + 1) * 128]
                if masked:
                    a = a * mask[s * RL + 2 * p].astype(F32)
                    b = b * mask[s * RL + 2 * p + 1].astype(F32)
                first, second = pair_lanes(a, b)
                pk[kind, 2 * hp, :, p * 128:(p + 1) * 128] = first.astype(BF)
                pk[kind, 2 * hp + 1, :, p * 128:(p + 1) * 128] = second.astype(BF)

    def over_y(kind, into, base, g):
        rows = chunk(base, CL)
        pushes = [
            Push(log, pk.at[kind, yidx[d] * HG + g], into.at[g, rows], (ys, yr), (kind, g, d - 1), ydev[d])
            for d in (2, 1, 3)
        ]
        into[g, rows, :] = pk[kind, y * HG + g]
        return pushes

    def spread(kind, ref, pushes, g):
        for p in pushes[g]:
            p.recv()
        block = ref.at[g, chunk(w, 256)]
        return (
            Push(log, block, block, (fs, fr), (kind, g, 0), far),
            Push(log, block, block, (fs, fr), (kind, g, 1), core),
        )

    def piece(index, i):
        block = kb.at[0, chunk(w * NY + index, CL)]
        return (
            Push(log, block, block, (ps, pr), (0, i), far),
            Push(log, block, block, (ps, pr), (1, i), core),
        )

    def join(pieces):
        for a, b in pieces:
            a.recv()
        block = kb.at[0, chunk(w_far, 256)]
        last = Push(log, block, block, (fs, fr), (0, 0, 2), core)
        for a, b in pieces:
            b.recv()
        return last

    def relay(kind, ref, pushes, g):
        pushes[0].recv()
        block = ref.at[g, chunk(w_far, 256)]
        last = Push(log, block, block, (fs, fr), (kind, g, 2), core)
        pushes[1].recv()
        return last

    def logits(g, last):
        for p in qy[g]:
            p.recv()
        last.recv()
        for j in range(4):
            block = dot(qb[g], kb[g, j * 256:(j + 1) * 256, :], ((1,), (1,)))
            part[g, :, j * 256:(j + 1) * 256] = block * (1.0 / 64.0)
        raw = part[g]
        e = jnp.exp(raw - jnp.max(raw, axis=-1, keepdims=True))
        center = jnp.sum(e * raw, axis=-1, keepdims=True) / jnp.sum(e, axis=-1, keepdims=True)
        shifted = raw - center
        part[g] = shifted
        pb[g] = shifted.astype(BF)
        return [
            Push(log, pb.at[g, chunk(zidx[d], 64)], rs.at[g, d - 1], (zs, zr), (g, d - 1), zdev[d]) for d in (2, 1, 3)
        ]

    def over_z(g, pushes):
        for p in pushes:
            p.recv()
        total = part[g, chunk(z, 64), :]
        for d in range(NZ - 1):
            total = total + rs[g, d].astype(F32)
        th[g] = total
        xs[g] = total.astype(BF)
        return Push(log, xs.at[g], xr.at[g], (hs, hr), (g,), xdev)

    def soften(g, push):
        push.recv()
        total = th[g] + xr[g].astype(F32)
        e = jnp.exp(total - jnp.max(total, axis=-1, keepdims=True))
        rows = chunk(z, 64)
        pw[g, rows, :] = (e / jnp.sum(e, axis=-1, keepdims=True)).astype(BF)
        block = pw.at[g, rows]
        return [
            Push(log, block, block, (as_, ar), (g, 0), zdev[1]),
            Push(log, block, block, (as_, ar), (g, 1), zdev[3]),
        ]

    def onward(g, pushes):
        pushes[0].recv()
        first = pw.at[g, chunk(zidx[3] * 2, 32)]
        a = Push(log, first, first, (as_, ar), (g, 2), zdev[1])
        pushes[1].recv()
        second = pw.at[g, chunk(zidx[1] * 2 + 1, 32)]
        b = Push(log, second, second, (as_, ar), (g, 3), zdev[3])
        return [a, b]

    def mix(g, last, pushes):
        last.recv()
        for p in pushes:
            p.recv()
        mxs[g] = dot(pw[g], vb[g]).astype(BF)
        got = [
            Push(log, mxs.at[g, chunk(yidx[d], CL)], mxr.at[y * HG + g], (ms, mr), (g, d - 1), ydev[d])
            for d in (2, 1, 3)
        ]
        mxr[y * HG + g] = mxs[g, chunk(y, CL), :]
        return got

    own = w * NY + y
    ky, qy, vy = [None] * HG, [None] * HG, [None] * HG
    project(0, wrk, loads[0])
    pl.semaphore_wait(barrier, len(peers))
    ky[0] = over_y(0, kb, own, 0)
    k0 = [piece(y, 0)]
    mask_load.wait()
    project(1, wrq, loads[1], masked=True)
    ky[1] = over_y(0, kb, own, 1)
    qy[0] = over_y(1, qb, y, 0)
    ky[2] = over_y(0, kb, own, 2)
    qy[1] = over_y(1, qb, y, 1)
    qy[2] = over_y(1, qb, y, 2)
    for push, d in ((ky[0][1], 3), (ky[0][2], 1), (ky[0][0], 2)):
        push.recv()
        k0.append(piece(yidx[d], d))
    project(2, wrv, loads[2])
    for g in range(HG):
        vy[g] = over_y(2, vb, own, g)
    k1 = spread(0, kb, ky, 1)
    k0 = join(k0)
    z0 = logits(0, k0)
    k2 = spread(0, kb, ky, 2)
    k1 = relay(0, kb, k1, 1)
    z1 = logits(1, k1)
    x0 = over_z(0, z0)
    k2 = relay(0, kb, k2, 2)
    v0 = spread(1, vb, vy, 0)
    z2 = logits(2, k2)
    p0 = soften(0, x0)
    x1 = over_z(1, z1)
    x2 = over_z(2, z2)
    v1 = spread(1, vb, vy, 1)
    v2 = spread(1, vb, vy, 2)
    p1 = soften(1, x1)
    p0 = onward(0, p0)
    v0 = relay(1, vb, v0, 0)
    p2 = soften(2, x2)
    m = mix(0, v0, p0)
    p1 = onward(1, p1)
    p2 = onward(2, p2)
    v1 = relay(1, vb, v1, 1)
    m = m + mix(1, v1, p1)
    v2 = relay(1, vb, v2, 2)
    m = m + mix(2, v2, p2)
    for p in m:
        p.recv()
    for p in range(RL // 2):
        for hp in range(H // 2):
            a = mxr[2 * hp, :, p * 128:(p + 1) * 128].astype(F32)
            b = mxr[2 * hp + 1, :, p * 128:(p + 1) * 128].astype(F32)
            first, second = pair_lanes(a, b)
            xn[2 * p * CL:(2 * p + 1) * CL, hp * 128:(hp + 1) * 128] = first.astype(BF)
            xn[(2 * p + 1) * CL:(2 * p + 2) * CL, hp * 128:(hp + 1) * 128] = second.astype(BF)
    loads[3].wait()
    for n in range(D // 256):
        wide = dot(xn[...], wro[:, n * 256:(n + 1) * 256])
        for j in (2 * n, 2 * n + 1):
            lanes = slice(j * 128, (j + 1) * 128)
            xf[j] = x[:, lanes].astype(F32) + wide[:, (j - 2 * n) * 128:(j - 2 * n + 1) * 128]

    c_in = []
    for half in range(2):
        for t in range(NS):
            for j in range(D // 128):
                tiles = [xf[j, pl.ds(t * 8 + half * 4 + k, RL, stride=CL), :] for k in range(4)]
                cs[half, t, :, j * 128:(j + 1) * 128] = jnp.concatenate(tiles, axis=0).astype(BF)
        c_in.append([
            Push(log, cs.at[half, sidx[d]], ci.at[half, s], (cs_s, cs_r), (half, d - 1), sdev[d])
            for d in (2, 6, 1, 3, 5, 7, 4)
        ])
        ci[half, s] = cs[half, s]

    row = lax.broadcasted_iota(jnp.int32, (8, 128), 0)
    for t in range(NS):
        tile = jnp.zeros((8, 128), F32)
        for k in range(8):
            tile = jnp.where(row == k, mask[t * 8 + k].astype(F32), tile)
        bias[t * 8:(t + 1) * 8, :] = tile
    live = jnp.concatenate([bias[...], bias[...]], axis=1) > 0.5
    lane = lax.broadcasted_iota(jnp.int32, (1, 256), 1)
    pick = [((lane >= h * 64) & (lane < (h + 1) * 64)).astype(F32) for h in range(4)]

    def attend(tiles):
        scores = []
        for rows, lanes in tiles:
            q = qc[rows, lanes]
            wide = jnp.concatenate([q * pick[h].astype(BF) for h in range(4)], axis=0)
            scores.append(dot(kc[rows, lanes], wide, ((1,), (1,))))
        weights = []
        for st in scores:
            st = jnp.where(live, st * 0.125, -1e30)
            e = jnp.exp(st - jnp.max(st, axis=0, keepdims=True))
            weights.append((e / jnp.sum(e, axis=0, keepdims=True)).astype(BF))
        for (rows, lanes), p in zip(tiles, weights):
            res = dot(p, vc[rows, lanes], ((0,), (0,)))
            mixed = res[0:64] * pick[0]
            for h in range(1, 4):
                mixed = mixed + res[h * 64:(h + 1) * 64] * pick[h]
            cin[rows, lanes] = mixed.astype(BF)

    back = []
    for half in range(2):
        for p in c_in[half]:
            p.recv()
        for k in range(4):
            xo[k * 64:(k + 1) * 64, :] = jnp.concatenate(
                [ci[half, t].astype(F32)[k * 8:(k + 1) * 8] for t in range(NS)], axis=0
            )
        cin[...] = norm(xo[...], gain(gc)).astype(BF)
        for load, weight, into in ((loads[4], wcq, qc), (loads[5], wck, kc), (loads[6], wcv, vc)):
            load.wait()
            into[...] = dot(cin[...], weight[...]).astype(BF)

        attend([(slice(c * 64, (c + 1) * 64), slice(g * 256, (g + 1) * 256)) for c in range(4) for g in range(3)])
        loads[7].wait()
        after = (xo[...] + dot(cin[...], wco[...])).astype(BF).astype(F32)
        facc[...] = after
        cin[...] = norm(after, gain(gf)).astype(BF)
        loads[8].wait()
        loads[9].wait()

        @pl.loop(0, FF // D)
        def _(n):
            part_n = chunk(n, D)
            h = dot(cin[...], up[:, part_n])
            hb[...] = (0.5 * h * (1.0 + lax.erf(h * 0.7071067811865476))).astype(BF)
            facc[...] += dot(hb[...], dn[part_n, :])

        for t in range(NS):
            tiles = [facc[k * 64 + t * 8:k * 64 + (t + 1) * 8, :] for k in range(4)]
            co[half, t] = jnp.concatenate(tiles, axis=0).astype(BF)
        back.append([
            Push(log, co.at[half, sidx[d]], cr.at[half, s], (os_, or_), (half, d - 1), sdev[d])
            for d in (2, 6, 1, 3, 5, 7, 4)
        ])
        cr[half, s] = co[half, s]
    for half in range(2):
        for p in back[half]:
            p.recv()
        for t in range(NS):
            for j in range(D // 128):
                wide = cr[half, t, :, j * 128:(j + 1) * 128].astype(F32)
                for k in range(4):
                    xf[j, pl.ds(t * 8 + half * 4 + k, RL, stride=CL), :] = wide[k * 8:(k + 1) * 8]
    for j in range(D // 128):
        out[:, j * 128:(j + 1) * 128] = xf[j].astype(BF)
    finish(log, loads)


def vmem():
    return pl.BlockSpec(memory_space=pltpu.VMEM)


def hbm():
    return pl.BlockSpec(memory_space=pl.ANY)


def pairs_of(*shape):
    return [pltpu.SemaphoreType.DMA(shape)] * 2


def local(
    stream, row_mask, gain_row, row_query, row_key, row_value, row_output,
    gain_column, column_query, column_key, column_value, column_output,
    gain_feed, up_weight, down_weight,
):
    def bf(*shape):
        return pltpu.VMEM(shape, BF)

    def f32(*shape):
        return pltpu.VMEM(shape, F32)

    out = pl.pallas_call(
        layer_kernel,
        out_shape=jax.ShapeDtypeStruct((T, D), BF),
        in_specs=[hbm()] + [vmem()] * 4 + [hbm()] * 10,
        out_specs=vmem(),
        scratch_shapes=[pltpu.SMEM((NS * RL,), jnp.int32)] + [bf(D, D)] * 8 + [
            bf(D, FF), bf(FF, D),
            bf(T, D), f32(T, D), bf(3, H, CL, 512),
            bf(HG, 256, 512), bf(HG, 1024, 512), bf(HG, 1024, 512),
            f32(HG, 256, 1024), bf(HG, 256, 1024), bf(HG, NZ - 1, 64, 1024),
            f32(HG, 64, 1024), bf(HG, 64, 1024), bf(HG, 64, 1024),
            bf(HG, 256, 1024), bf(HG, 256, 512), bf(H, CL, 512),
            bf(2, NS, 32, D), bf(2, NS, 32, D),
            f32(D // 128, T, 128), f32(256, D), bf(256, D), bf(256, D), bf(256, D), bf(256, D), bf(256, D),
            f32(256, D), bf(2, NS, 32, D), bf(2, NS, 32, D), f32(64, 128),
            pltpu.SemaphoreType.DMA((11,)),
        ] + pairs_of(3, HG, NY - 1) + pairs_of(2, HG, 3) + pairs_of(2, NY) + pairs_of(HG, NZ - 1)
        + pairs_of(HG) + pairs_of(HG, 4) + pairs_of(HG, NY - 1) + pairs_of(2, NS - 1) + pairs_of(2, NS - 1),
        compiler_params=pltpu.CompilerParams(
            collective_id=0, has_side_effects=True, vmem_limit_bytes=VMEM_LIMIT
        ),
        name="layer",
    )(
        row_mask, stream.reshape(T, D), gain_row, gain_column, gain_feed,
        row_query, row_key, row_value, row_output,
        column_query, column_key, column_value, column_output, up_weight, down_weight,
    )
    return out.reshape(RL, CL, D)


def solution(mesh):
    return jax.shard_map(
        local,
        mesh=mesh,
        in_specs=(P("seq", "col", None),) + (P(),) * 14,
        out_specs=P("seq", "col", None),
        check_vma=False,
    )
```
